128 devices in a mesh: ops: 4 (over z), sec: 32 (over y, x, core).
Axes of the slice: x: 4, y: 4, z: 4, core: 2. Of those that a mesh axis runs over, the one named last changes fastest.
Arguments:
- psi_blocks: bfloat16 [32, 16, 512, 512], P('sec'), may hold values from -6 to 6
- left_env: bfloat16 [4, 32, 512, 512], P('ops', 'sec'), may hold values from -0.25 to 0.25
- right_env: bfloat16 [4, 32, 512, 512], P('ops', 'sec'), may hold values from -0.25 to 0.25
- shifts: int32 [16], replicated, may hold values from 0 to 31, as said below
- sector_dims: int32 [32], replicated, may hold values from 64 to 512, as said below
Outputs:
- sigma_blocks: bfloat16 [32, 16, 512, 512], P('sec', 'ops')
The draws below stay inside these ranges and needn't reach their ends.
Inputs may be any that keep to these rules, and one draw needn't show every extreme that they name: `shifts`: the values are distinct; 0, 1, 16 and 31 are among them. `sector_dims`: one sector has exactly 512 live states.
All inputs are finite; a program needn't handle non-finite values.
Results may differ from the reference program's by a relative error of at most 0.013.
Values may be sent and summed in bfloat16 or wider, within the bound.
A program may use at most 128 MiB of HBM per device.

```python
import jax
import jax.numpy as jnp
from jax import lax

M = 512
SECTORS = 32
PARTNERS = 16
TERMS = 4
N_OPS = 4


def draw_shifts(key, part):
    key = jax.random.fold_in(key, 2)
    first_key, second_key = jax.random.split(key)
    half_point = SECTORS // 2
    candidates = jnp.arange(SECTORS - 4, dtype=jnp.int32) + 2
    candidates = candidates + (candidates >= half_point).astype(jnp.int32)
    inner = jax.random.permutation(first_key, candidates)[:PARTNERS - 4]
    values = jnp.concatenate([jnp.array([0, 1, half_point, SECTORS - 1], jnp.int32), inner.astype(jnp.int32)])
    order = jax.random.permutation(second_key, PARTNERS)
    return values[order].astype(jnp.int32)


def draw_sector_dims(key, part):
    key = jax.random.fold_in(key, 1)
    first_key, second_key = jax.random.split(key)
    values = jax.random.randint(first_key, (SECTORS,), M // 8, M + 1).astype(jnp.int32)
    chosen = jax.random.randint(second_key, (), 0, SECTORS).astype(jnp.int32)
    return jnp.where(jnp.arange(SECTORS, dtype=jnp.int32) == chosen, M, values).astype(jnp.int32)


def level_of(own_key, extent, pieces, smallest, high):
    gain = 1.0
    for axis_at, parts in pieces:
        steps = jax.random.uniform(jax.random.fold_in(jax.random.fold_in(own_key, 6), axis_at), (parts,), jnp.float32, smallest / len(pieces), high / len(pieces))
        gain = gain * jnp.repeat(jnp.exp(steps), extent[axis_at] // parts).reshape((-1,) + (1,) * (len(extent) - 1 - axis_at))
    return gain


def gaussian(key, shape, scale, reach, shards=(), kind=jnp.bfloat16):
    entries = scale * jax.random.normal(key, shape, jnp.float32)
    if shards:
        entries = entries * level_of(key, shape, shards, -0.22, 0.18)
    return jnp.clip(entries, -reach, reach).astype(kind)


def setup_inputs(seed: int = 0) -> dict:
    splits = jax.random.split(jax.random.key(seed), 6)
    return {
        "psi_blocks": gaussian(splits[0], (SECTORS, PARTNERS, M, M), 1.0, 6.0, ((0, 32),)),
        "left_env": gaussian(splits[1], (TERMS, SECTORS, M, M), M ** -0.5, 0.25, ((0, 4), (1, 32))),
        "right_env": gaussian(splits[2], (TERMS, SECTORS, M, M), M ** -0.5, 0.25, ((0, 4), (1, 32))),
        "shifts": draw_shifts(jax.random.fold_in(splits[5], 71), 0),
        "sector_dims": draw_sector_dims(jax.random.fold_in(splits[5], 71), 0),
    }


def reference(psi_blocks, left_env, right_env, shifts, sector_dims):
    sectors = psi_blocks.shape[0]
    partners = psi_blocks.shape[1]
    block_width = psi_blocks.shape[2]
    terms = left_env.shape[0]
    groups = N_OPS
    per_group = terms // groups
    positions = jnp.arange(block_width, dtype=jnp.int32)
    slot_ids = jnp.arange(partners, dtype=jnp.int32)

    def one_sector(sector):
        anchor = jnp.mod(sector - shifts, sectors).astype(jnp.int32)
        blocks = psi_blocks[anchor, slot_ids]
        row_mask = positions[None, :] < sector_dims[anchor][:, None]
        col_mask = positions < sector_dims[sector]
        full_mask = row_mask[:, :, None] & col_mask[None, None, :]
        blocks = jnp.where(full_mask, blocks, jnp.zeros((), jnp.bfloat16))
        left_sel = left_env[:, anchor]
        halfway = jnp.einsum('tpij,pjk->tpik', left_sel.astype(jnp.float32), blocks.astype(jnp.float32)).astype(jnp.bfloat16)
        right_blocks = right_env[:, sector]
        product = jnp.einsum('tpik,tkl->tpil', halfway.astype(jnp.float32), right_blocks.astype(jnp.float32))
        partial_value = product.reshape(groups, per_group, partners, block_width, block_width).sum(axis=1)
        partial_value = lax.optimization_barrier(partial_value.astype(jnp.bfloat16)).astype(jnp.float32)
        totals = partial_value.sum(axis=0)
        totals = jnp.where(full_mask, totals, jnp.zeros((), totals.dtype))
        return totals.astype(jnp.bfloat16)

    return lax.map(one_sector, jnp.arange(sectors, dtype=jnp.int32))
```

```python
import functools

import jax
import jax.numpy as jnp
from jax import lax
from jax.experimental import pallas as pl
from jax.experimental.pallas import tpu as pltpu
from jax.sharding import PartitionSpec as P

MESH = pl.DeviceIdType.MESH
BF16 = jnp.bfloat16
F32 = jnp.float32

M = 512
W = 128
C = M // W
NP = 16
H = W // 2

AG0, AG1, AG2, AG3, SIB = 0, 4, 8, 12, 16
RS, SWAP, A1, A2, ZOUT = 24, 30, 31, 37, 43
EVENTS = 46


class Copy:
    def __init__(self, make):
        self.make = make

    def start(self):
        self.make().start()

    def wait_send(self):
        self.make().wait_send()

    def wait_recv(self):
        self.make().wait_recv()


def kernel(shifts, dims, psi, left, right, out,
           inter, lmask, part, rsin, sigma, v, w, x0, x1, zbuf, inv,
           psem, osem, ssem, rsem, *chunked):
    rall, yf = chunked[:C], chunked[C:]
    g = lax.axis_index("ops")
    s = lax.axis_index("sec")
    y, x, c = s // 8, (s // 2) % 4, s % 2

    def dev(dz=0, dy=0, dx=0, dc=0):
        return ((g + dz) % 4, ((y + dy) % 4) * 8 + ((x + dx) % 4) * 2 + (c + dc) % 2)

    def copy(i, e, src, dst, to):
        return Copy(lambda: pltpu.make_async_remote_copy(
            src_ref=src, dst_ref=dst, send_sem=ssem.at[i, e], recv_sem=rsem.at[i, e],
            device_id=to, device_id_type=MESH))

    gp, gm, go = (g + 1) % 4, (g + 3) % 4, (g + 2) % 4
    xp, xm, xo = (x + 1) % 4, (x + 3) % 4, (x + 2) % 4
    yp, ym, yo = (y + 1) % 4, (y + 3) % 4, (y + 2) % 4
    XP, XM, YP, YM = dev(dx=1), dev(dx=3), dev(dy=1), dev(dy=3)
    ZP, ZM = dev(dz=1), dev(dz=3)
    SB = dev(dc=1)

    def ag0(i):
        a = rall[i].at[y, x, c, pl.ds(0, 256)]
        b = rall[i].at[y, x, c, pl.ds(256, 256)]
        return [copy(i, AG0, a, a, XP), copy(i, AG0 + 1, a, a, XM),
                copy(i, AG0 + 2, b, b, YP), copy(i, AG0 + 3, b, b, YM)]

    def ag1(i):
        q = [rall[i].at[y, xm, c, pl.ds(0, 128)], rall[i].at[y, xp, c, pl.ds(128, 128)],
             rall[i].at[ym, x, c, pl.ds(256, 128)], rall[i].at[yp, x, c, pl.ds(384, 128)]]
        return [copy(i, AG1 + k, r, r, to) for k, (r, to) in enumerate(zip(q, (XP, XM, YP, YM)))]

    def ag2(i):
        a = rall[i].at[y, :, c, pl.ds(0, 256)]
        b = rall[i].at[:, x, c, pl.ds(256, 256)]
        return [copy(i, AG2, a, a, YP), copy(i, AG2 + 1, a, a, YM),
                copy(i, AG2 + 2, b, b, XP), copy(i, AG2 + 3, b, b, XM)]

    def ag3(i):
        q = [rall[i].at[ym, :, c, pl.ds(0, 128)], rall[i].at[yp, :, c, pl.ds(128, 128)],
             rall[i].at[:, xm, c, pl.ds(256, 128)], rall[i].at[:, xp, c, pl.ds(384, 128)]]
        return [copy(i, AG3 + k, r, r, to) for k, (r, to) in enumerate(zip(q, (YP, YM, XP, XM)))]

    def sib(i):
        q = [rall[i].at[r, :, c, pl.ds(0, 256)] for r in (y, ym, yp, yo)]
        t = [rall[i].at[:, r, c, pl.ds(256, 256)] for r in (x, xm, xp, xo)]
        return [copy(i, SIB + k, r, r, SB) for k, r in enumerate(q + t)]

    def start(cs):
        for cp in cs:
            cp.start()

    def arrive(cs):
        for cp in cs:
            cp.wait_recv()

    def sent(cs):
        for cp in cs:
            cp.wait_send()

    def gather_step1(i):
        arrive(ag0(i))
        start(ag1(i))

    def gather_step2(i):
        arrive(ag1(i))
        start(ag2(i))
        cs = sib(i)
        start([cs[0], cs[4]])

    def gather_step3(i):
        arrive(ag2(i))
        start(ag3(i))
        cs = sib(i)
        start([cs[1], cs[2], cs[5], cs[6]])

    def gather_step4(i):
        arrive(ag3(i))
        cs = sib(i)
        start([cs[3], cs[7]])

    lo, hi = pl.ds(0, 8), pl.ds(8, 8)

    def rs(i):
        b = i % 2
        return [copy(i, RS, part.at[b, go, lo], rsin.at[i, 0], ZM),
                copy(i, RS + 1, part.at[b, go, hi], rsin.at[i, 1], ZP),
                copy(i, RS + 2, part.at[b, gp, lo], rsin.at[i, 2], ZP),
                copy(i, RS + 3, part.at[b, gm, hi], rsin.at[i, 3], ZM),
                copy(i, RS + 4, part.at[b, gm, lo], rsin.at[i, 4], ZM),
                copy(i, RS + 5, part.at[b, gp, hi], rsin.at[i, 5], ZP)]

    def products(i, first):
        b = i % 2

        @pl.loop(first, first + 8)
        def _(p):
            t = (s + shifts[p]) % 32
            r = jnp.dot(inter[p], rall[i][t // 8, (t // 2) % 4, t % 2], preferred_element_type=F32)
            r = r.astype(BF16)
            for d in range(4):
                part[b, d, p] = r[d * W:(d + 1) * W]

    def add_and_pass(i):
        b = i % 2
        cs = rs(i)
        cs[0].wait_recv()

        @pl.loop(0, 8)
        def _(p):
            part[b, gm, p] = (part[b, gm, p].astype(F32) + rsin[i, 0, p].astype(F32)).astype(BF16)

        cs[4].start()
        cs[1].wait_recv()

        @pl.loop(0, 8)
        def _(p):
            part[b, gp, p + 8] = (part[b, gp, p + 8].astype(F32) + rsin[i, 1, p].astype(F32)).astype(BF16)

        cs[5].start()

    def swap(i):
        return copy(i, SWAP, w.at[i], v.at[i, c], SB)

    def finish_sum(i):
        b = i % 2
        cs = rs(i)
        arrive(cs[2:])

        @pl.loop(0, 8)
        def _(p):
            sigma[p] = (part[b, g, p].astype(F32) + rsin[i, 2, p].astype(F32)
                        + rsin[i, 4, p].astype(F32)).astype(BF16)
            sigma[p + 8] = (part[b, g, p + 8].astype(F32) + rsin[i, 3, p].astype(F32)
                            + rsin[i, 5, p].astype(F32)).astype(BF16)

        @pl.loop(0, 16)
        def _(t):
            ty, tx = t // 4, t % 4
            base = ty * 8 + tx * 2 - s + 32
            w[i, ty, tx] = sigma[inv[(base + (c + 1) % 2) % 32]]
            v[i, c, ty, tx] = sigma[inv[(base + c) % 32]]

        swap(i).start()
        sent(cs)

    def a1(i):
        cs = []
        for d in (1, 3, 2):
            tx, ty = (x + d) % 4, (y + d) % 4
            cs.append(copy(i, A1 + d - 1, v.at[i, :, :, tx, pl.ds(0, H)], x0.at[i, x], dev(dx=d)))
            cs.append(copy(i, A1 + d + 2, v.at[i, :, ty, :, pl.ds(H, H)], x1.at[i, y], dev(dy=d)))
        return cs

    def a2(i):
        cs = []
        for d in (1, 3, 2):
            tx, ty = (x + d) % 4, (y + d) % 4
            cs.append(copy(i, A2 + d - 1, x0.at[i, :, :, ty], yf[i].at[y, :, :, pl.ds(0, H)], dev(dy=d)))
            cs.append(copy(i, A2 + d + 2, x1.at[i, :, :, tx], yf[i].at[:, x, :, pl.ds(H, H)], dev(dx=d)))
        return cs

    def exchange1(i):
        swap(i).wait_recv()
        start(a1(i))
        for k in range(4):
            for q in range(2):
                x0[i, x, q, k] = v[i, q, k, x, pl.ds(0, H)]
                x1[i, y, q, k] = v[i, q, y, k, pl.ds(H, H)]

    def exchange2(i):
        arrive(a1(i))
        start(a2(i))
        for k in range(4):
            for q in range(2):
                yf[i][y, k, q, pl.ds(0, H)] = x0[i, k, q, y]
                yf[i][k, x, q, pl.ds(H, H)] = x1[i, k, q, x]

    def place(i):
        return out.at[:, pl.ds(pl.multiple_of(g * W, W), W), pl.ds(i * W, W)]

    def zout(i):
        return [copy(i, ZOUT + d - 1, zbuf.at[i, (g + d) % 4], place(i), dev(dz=d)) for d in (2, 1, 3)]

    def own_out(i):
        return pltpu.make_async_copy(zbuf.at[i, g], place(i), osem.at[i])

    def exchange3(i):
        arrive(a2(i))

        @pl.loop(0, NP)
        def _(p):
            a = (s - shifts[p] + 32) % 32
            zbuf[i, p // 4, p % 4] = yf[i][a // 8, (a // 2) % 4, a % 2]

        start(zout(i))
        own_out(i).start()

    barrier = pltpu.get_barrier_semaphore()
    peers = ([dev(dz=d) for d in (1, 2, 3)] + [dev(dy=d) for d in (1, 2, 3)]
             + [dev(dx=d) for d in (1, 2, 3)] + [SB])
    for to in peers:
        pl.semaphore_signal(barrier, inc=1, device_id=to, device_id_type=MESH)

    def psi_copy(p):
        return pltpu.make_async_copy(psi.at[p], inter.at[p], psem.at[p])

    @pl.loop(0, NP)
    def _(p):
        psi_copy(p).start()

    own = dims[s]
    rows = lax.broadcasted_iota(jnp.int32, (M, W), 0)
    cols = lax.broadcasted_iota(jnp.int32, (M, W), 1)
    for i in range(C):
        live = (rows < own) & (cols + i * W < own)
        rall[i][y, x, c] = jnp.where(live, right[:, i * W:(i + 1) * W].astype(F32), 0.0).astype(BF16)
    pl.semaphore_wait(barrier, len(peers))
    start(ag0(0))
    for i in range(C):
        live = (rows < own) & (cols + i * W < own)
        lmask[:, i * W:(i + 1) * W] = jnp.where(live, left[:, i * W:(i + 1) * W].astype(F32), 0.0).astype(BF16)
    start(ag0(1))

    def find(k):
        r = jnp.int32(0)
        for p in range(NP):
            r = jnp.where(shifts[p] == k, jnp.int32(p), r)
        return r

    @pl.loop(0, 32)
    def _(k):
        inv[k] = find(k)

    def left_products(first, count):
        @pl.loop(first, first + count)
        def _(p):
            psi_copy(p).wait()
            for n in range(2):
                inter[p, :, n * 256:(n + 1) * 256] = jnp.dot(
                    lmask[...], inter[p, :, n * 256:(n + 1) * 256],
                    preferred_element_type=F32).astype(BF16)

    def g0(i):
        start(ag0(i))

    def lp(i):
        left_products(4 * i, 4)

    def pr(i):
        arrive(sib(i))
        products(i, 0)
        cs = rs(i)
        start([cs[0], cs[2]])
        products(i, 8)
        start([cs[1], cs[3]])

    g1, g2, g3, g4 = gather_step1, gather_step2, gather_step3, gather_step4
    ad, fi, e1, e2, e3 = add_and_pass, finish_sum, exchange1, exchange2, exchange3
    order = (
        (lp, 0), (g1, 0), (lp, 1), (g2, 0), (lp, 2), (g3, 0), (g1, 1), (lp, 3), (g2, 1), (g4, 0),
        (pr, 0), (g0, 2), (g3, 1), (g1, 2), (ad, 0), (g4, 1), (g2, 2), (pr, 1), (fi, 0),
        (g3, 2), (e1, 0), (ad, 1), (g4, 2), (e2, 0), (pr, 2), (g0, 3), (g1, 3), (fi, 1),
        (e3, 0), (e1, 1), (g2, 3), (ad, 2), (e2, 1), (g3, 3), (g4, 3), (pr, 3), (fi, 2),
        (e3, 1), (e1, 2), (ad, 3), (e2, 2), (fi, 3), (e3, 2), (e1, 3), (e2, 3), (e3, 3),
    )
    for step, i in order:
        step(i)

    for i in range(C):
        arrive(zout(i))
        own_out(i).wait()
        sent(ag0(i) + ag1(i) + ag2(i) + ag3(i) + sib(i) + [swap(i)] + a1(i) + a2(i) + zout(i))


def body(psi_blocks, left_env, right_env, shifts, sector_dims):
    vmem = pl.BlockSpec(memory_space=pltpu.VMEM)
    smem = pl.BlockSpec(memory_space=pltpu.SMEM)
    hbm = pl.BlockSpec(memory_space=pl.ANY)
    out = pl.pallas_call(
        kernel,
        name="sigma",
        out_shape=jax.ShapeDtypeStruct((4, M, M), BF16),
        in_specs=[smem, smem, hbm, vmem, vmem],
        out_specs=hbm,
        scratch_shapes=[
            pltpu.VMEM((NP, M, M), BF16),
            pltpu.VMEM((M, M), BF16),
            pltpu.VMEM((2, 4, NP, W, W), BF16),
            pltpu.VMEM((C, 6, 8, W, W), BF16),
            pltpu.VMEM((NP, W, W), BF16),
            pltpu.VMEM((C, 2, 4, 4, W, W), BF16),
            pltpu.VMEM((C, 4, 4, W, W), BF16),
            pltpu.VMEM((C, 4, 2, 4, H, W), BF16),
            pltpu.VMEM((C, 4, 2, 4, H, W), BF16),
            pltpu.VMEM((C, 4, 4, W, W), BF16),
            pltpu.SMEM((32,), jnp.int32),
            pltpu.SemaphoreType.DMA((NP,)),
            pltpu.SemaphoreType.DMA((C,)),
            pltpu.SemaphoreType.DMA((C, EVENTS)),
            pltpu.SemaphoreType.DMA((C, EVENTS)),
            *[pltpu.VMEM((4, 4, 2, M, W), BF16)] * C,
            *[pltpu.VMEM((4, 4, 2, W, W), BF16)] * C,
        ],
        compiler_params=pltpu.CompilerParams(
            collective_id=1, has_side_effects=True, vmem_limit_bytes=60 << 20),
        cost_estimate=pl.CostEstimate(flops=2 * 32 * M ** 3, bytes_accessed=12 << 20, transcendentals=0),
    )(shifts, sector_dims, psi_blocks[0], left_env[0, 0], right_env[0, 0])
    return out[None]


def solution(mesh):
    in_specs = (
        P("sec", None, None, None),
        P("ops", "sec", None, None),
        P("ops", "sec", None, None),
        P(),
        P(),
    )
    out_specs = P("sec", "ops", None, None)
    return jax.shard_map(body, mesh=mesh, in_specs=in_specs, out_specs=out_specs, check_vma=False)
```

```python
import functools

import jax
import jax.numpy as jnp
from jax import lax
from jax.experimental import pallas as pl
from jax.experimental.pallas import tpu as pltpu
from jax.sharding import PartitionSpec as P

MESH = pl.DeviceIdType.MESH
BF16 = jnp.bfloat16
F32 = jnp.float32

M = 512
W = 128
C = M // W
NP = 16
H = W // 2

AG0, AG1, AG2, AG3, SIB = 0, 4, 8, 12, 16
RS, SWAP, A1, A2, ZOUT = 24, 30, 31, 37, 43
EVENTS = 46


class Copy:
    def __init__(self, make):
        self.make = make

    def start(self):
        self.make().start()

    def wait_send(self):
        self.make().wait_send()

    def wait_recv(self):
        self.make().wait_recv()


def kernel(shifts, dims, psi, left, right, out,
           inter, lmask, part, rsin, sigma, v, w, x0, x1, zbuf, inv,
           psem, osem, ssem, rsem, *chunked):
    rall, yf = chunked[:C], chunked[C:]
    g = lax.axis_index("ops")
    s = lax.axis_index("sec")
    y, x, c = s // 8, (s // 2) % 4, s % 2

    def dev(dz=0, dy=0, dx=0, dc=0):
        return ((g + dz) % 4, ((y + dy) % 4) * 8 + ((x + dx) % 4) * 2 + (c + dc) % 2)

    def copy(i, e, src, dst, to):
        return Copy(lambda: pltpu.make_async_remote_copy(
            src_ref=src, dst_ref=dst, send_sem=ssem.at[i, e], recv_sem=rsem.at[i, e],
            device_id=to, device_id_type=MESH))

    gp, gm, go = (g + 1) % 4, (g + 3) % 4, (g + 2) % 4
    xp, xm, xo = (x + 1) % 4, (x + 3) % 4, (x + 2) % 4
    yp, ym, yo = (y + 1) % 4, (y + 3) % 4, (y + 2) % 4
    XP, XM, YP, YM = dev(dx=1), dev(dx=3), dev(dy=1), dev(dy=3)
    ZP, ZM = dev(dz=1), dev(dz=3)
    SB = dev(dc=1)

    def ag0(i):
        a = rall[i].at[y, x, c, pl.ds(0, 256)]
        b = rall[i].at[y, x, c, pl.ds(256, 256)]
        return [copy(i, AG0, a, a, XP), copy(i, AG0 + 1, a, a, XM),
                copy(i, AG0 + 2, b, b, YP), copy(i, AG0 + 3, b, b, YM)]

    def ag1(i):
        q = [rall[i].at[y, xm, c, pl.ds(0, 128)], rall[i].at[y, xp, c, pl.ds(128, 128)],
             rall[i].at[ym, x, c, pl.ds(256, 128)], rall[i].at[yp, x, c, pl.ds(384, 128)]]
        return [copy(i, AG1 + k, r, r, to) for k, (r, to) in enumerate(zip(q, (XP, XM, YP, YM)))]

    def ag2(i):
        a = rall[i].at[y, :, c, pl.ds(0, 256)]
        b = rall[i].at[:, x, c, pl.ds(256, 256)]
        return [copy(i, AG2, a, a, YP), copy(i, AG2 + 1, a, a, YM),
                copy(i, AG2 + 2, b, b, XP), copy(i, AG2 + 3, b, b, XM)]

    def ag3(i):
        q = [rall[i].at[ym, :, c, pl.ds(0, 128)], rall[i].at[yp, :, c, pl.ds(128, 128)],
             rall[i].at[:, xm, c, pl.ds(256, 128)], rall[i].at[:, xp, c, pl.ds(384, 128)]]
        return [copy(i, AG3 + k, r, r, to) for k, (r, to) in enumerate(zip(q, (YP, YM, XP, XM)))]

    def sib(i):
        q = [rall[i].at[r, :, c, pl.ds(0, 256)] for r in (y, ym, yp, yo)]
        t = [rall[i].at[:, r, c, pl.ds(256, 256)] for r in (x, xm, xp, xo)]
        return [copy(i, SIB + k, r, r, SB) for k, r in enumerate(q + t)]

    def start(cs):
        for cp in cs:
            cp.start()

    def arrive(cs):
        for cp in cs:
            cp.wait_recv()

    def sent(cs):
        for cp in cs:
            cp.wait_send()

    def gather_step1(i):
        arrive(ag0(i))
        start(ag1(i))

    def gather_step2(i):
        arrive(ag1(i))
        start(ag2(i))
        cs = sib(i)
        start([cs[0], cs[4]])

    def gather_step3(i):
        arrive(ag2(i))
        start(ag3(i))
        cs = sib(i)
        start([cs[1], cs[2], cs[5], cs[6]])

    def gather_step4(i):
        arrive(ag3(i))
        cs = sib(i)
        start([cs[3], cs[7]])

    lo, hi = pl.ds(0, 8), pl.ds(8, 8)

    def rs(i):
        b = i % 2
        return [copy(i, RS, part.at[b, go, lo], rsin.at[i, 0], ZM),
                copy(i, RS + 1, part.at[b, go, hi], rsin.at[i, 1], ZP),
                copy(i, RS + 2, part.at[b, gp, lo], rsin.at[i, 2], ZP),
                copy(i, RS + 3, part.at[b, gm, hi], rsin.at[i, 3], ZM),
                copy(i, RS + 4, part.at[b, gm, lo], rsin.at[i, 4], ZM),
                copy(i, RS + 5, part.at[b, gp, hi], rsin.at[i, 5], ZP)]

    def products(i, first):
        b = i % 2

        @pl.loop(first, first + 8, unroll=8)
        def _(p):
            t = (s + shifts[p]) % 32
            r = jnp.dot(inter[p], rall[i][t // 8, (t // 2) % 4, t % 2], preferred_element_type=F32)
            r = r.astype(BF16)
            for d in range(4):
                part[b, d, p] = r[d * W:(d + 1) * W]

    def add_and_pass(i):
        b = i % 2
        cs = rs(i)
        cs[0].wait_recv()

        @pl.loop(0, 8)
        def _(p):
            part[b, gm, p] = (part[b, gm, p].astype(F32) + rsin[i, 0, p].astype(F32)).astype(BF16)

        cs[4].start()
        cs[1].wait_recv()

        @pl.loop(0, 8)
        def _(p):
            part[b, gp, p + 8] = (part[b, gp, p + 8].astype(F32) + rsin[i, 1, p].astype(F32)).astype(BF16)

        cs[5].start()

    def swap(i):
        return copy(i, SWAP, w.at[i], v.at[i, c], SB)

    def finish_sum(i):
        b = i % 2
        cs = rs(i)
        arrive(cs[2:])

        @pl.loop(0, 8)
        def _(p):
            sigma[p] = (part[b, g, p].astype(F32) + rsin[i, 2, p].astype(F32)
                        + rsin[i, 4, p].astype(F32)).astype(BF16)
            sigma[p + 8] = (part[b, g, p + 8].astype(F32) + rsin[i, 3, p].astype(F32)
                            + rsin[i, 5, p].astype(F32)).astype(BF16)

        @pl.loop(0, 16)
        def _(t):
            ty, tx = t // 4, t % 4
            base = ty * 8 + tx * 2 - s + 32
            w[i, ty, tx] = sigma[inv[(base + (c + 1) % 2) % 32]]
            v[i, c, ty, tx] = sigma[inv[(base + c) % 32]]

        swap(i).start()
        sent(cs)

    def a1(i):
        cs = []
        for d in (1, 3, 2):
            tx, ty = (x + d) % 4, (y + d) % 4
            cs.append(copy(i, A1 + d - 1, v.at[i, :, :, tx, pl.ds(0, H)], x0.at[i, x], dev(dx=d)))
            cs.append(copy(i, A1 + d + 2, v.at[i, :, ty, :, pl.ds(H, H)], x1.at[i, y], dev(dy=d)))
        return cs

    def a2(i):
        cs = []
        for d in (1, 3, 2):
            tx, ty = (x + d) % 4, (y + d) % 4
            cs.append(copy(i, A2 + d - 1, x0.at[i, :, :, ty], yf[i].at[y, :, :, pl.ds(0, H)], dev(dy=d)))
            cs.append(copy(i, A2 + d + 2, x1.at[i, :, :, tx], yf[i].at[:, x, :, pl.ds(H, H)], dev(dx=d)))
        return cs

    def exchange1(i):
        swap(i).wait_recv()
        start(a1(i))
        for k in range(4):
            for q in range(2):
                x0[i, x, q, k] = v[i, q, k, x, pl.ds(0, H)]
                x1[i, y, q, k] = v[i, q, y, k, pl.ds(H, H)]

    def exchange2(i):
        arrive(a1(i))
        start(a2(i))
        for k in range(4):
            for q in range(2):
                yf[i][y, k, q, pl.ds(0, H)] = x0[i, k, q, y]
                yf[i][k, x, q, pl.ds(H, H)] = x1[i, k, q, x]

    def place(i):
        return out.at[:, pl.ds(pl.multiple_of(g * W, W), W), pl.ds(i * W, W)]

    def zout(i):
        return [copy(i, ZOUT + d - 1, zbuf.at[i, (g + d) % 4], place(i), dev(dz=d)) for d in (2, 1, 3)]

    def own_out(i):
        return pltpu.make_async_copy(zbuf.at[i, g], place(i), osem.at[i])

    def exchange3(i):
        arrive(a2(i))

        @pl.loop(0, NP)
        def _(p):
            a = (s - shifts[p] + 32) % 32
            zbuf[i, p // 4, p % 4] = yf[i][a // 8, (a // 2) % 4, a % 2]

        start(zout(i))
        own_out(i).start()

    barrier = pltpu.get_barrier_semaphore()
    peers = ([dev(dz=d) for d in (1, 2, 3)] + [dev(dy=d) for d in (1, 2, 3)]
             + [dev(dx=d) for d in (1, 2, 3)] + [SB])
    for to in peers:
        pl.semaphore_signal(barrier, inc=1, device_id=to, device_id_type=MESH)

    def psi_copy(p):
        return pltpu.make_async_copy(psi.at[p], inter.at[p], psem.at[p])

    @pl.loop(0, NP)
    def _(p):
        psi_copy(p).start()

    own = dims[s]
    rows = lax.broadcasted_iota(jnp.int32, (M, W), 0)
    cols = lax.broadcasted_iota(jnp.int32, (M, W), 1)
    for i in range(C):
        live = (rows < own) & (cols + i * W < own)
        rall[i][y, x, c] = jnp.where(live, right[:, i * W:(i + 1) * W].astype(F32), 0.0).astype(BF16)
    pl.semaphore_wait(barrier, len(peers))
    start(ag0(0))
    for i in range(C):
        live = (rows < own) & (cols + i * W < own)
        lmask[:, i * W:(i + 1) * W] = jnp.where(live, left[:, i * W:(i + 1) * W].astype(F32), 0.0).astype(BF16)
    start(ag0(1))

    def find(k):
        r = jnp.int32(0)
        for p in range(NP):
            r = jnp.where(shifts[p] == k, jnp.int32(p), r)
        return r

    @pl.loop(0, 32)
    def _(k):
        inv[k] = find(k)

    def left_products(first, count):
        @pl.loop(first, first + count)
        def _(p):
            psi_copy(p).wait()
            for n in range(2):
                inter[p, :, n * 256:(n + 1) * 256] = jnp.dot(
                    lmask[...], inter[p, :, n * 256:(n + 1) * 256],
                    preferred_element_type=F32).astype(BF16)

    def g0(i):
        start(ag0(i))

    def lp(i):
        left_products(4 * i, 4)

    def pr(i):
        arrive(sib(i))
        products(i, 0)
        cs = rs(i)
        start([cs[0], cs[2]])
        products(i, 8)
        start([cs[1], cs[3]])

    g1, g2, g3, g4 = gather_step1, gather_step2, gather_step3, gather_step4
    ad, fi, e1, e2, e3 = add_and_pass, finish_sum, exchange1, exchange2, exchange3
    order = (
        (lp, 1), (g1, 0), (g0, 2), (lp, 3), (g2, 0), (g1, 1), (g1, 2), (g3, 0), (lp, 2),
        (lp, 0), (g4, 0), (g2, 1), (g2, 2), (pr, 0), (g3, 1), (g0, 3), (ad, 0), (g1, 3),
        (g4, 1), (g3, 2), (pr, 1), (g4, 2), (fi, 0), (e1, 0), (g2, 3), (pr, 2), (g3, 3),
        (ad, 1), (g4, 3), (e2, 0), (ad, 2), (fi, 1), (pr, 3), (e1, 1), (fi, 2), (e1, 2),
        (e2, 1), (ad, 3), (e2, 2), (fi, 3), (e3, 0), (e1, 3), (e3, 2), (e2, 3), (e3, 1),
        (e3, 3),
    )
    for step, i in order:
        step(i)

    for i in range(C):
        arrive(zout(i))
        own_out(i).wait()
        sent(ag0(i) + ag1(i) + ag2(i) + ag3(i) + sib(i) + [swap(i)] + a1(i) + a2(i) + zout(i))


def body(psi_blocks, left_env, right_env, shifts, sector_dims):
    vmem = pl.BlockSpec(memory_space=pltpu.VMEM)
    smem = pl.BlockSpec(memory_space=pltpu.SMEM)
    hbm = pl.BlockSpec(memory_space=pl.ANY)
    out = pl.pallas_call(
        kernel,
        name="sigma",
        out_shape=jax.ShapeDtypeStruct((4, M, M), BF16),
        in_specs=[smem, smem, hbm, vmem, vmem],
        out_specs=hbm,
        scratch_shapes=[
            pltpu.VMEM((NP, M, M), BF16),
            pltpu.VMEM((M, M), BF16),
            pltpu.VMEM((2, 4, NP, W, W), BF16),
            pltpu.VMEM((C, 6, 8, W, W), BF16),
            pltpu.VMEM((NP, W, W), BF16),
            pltpu.VMEM((C, 2, 4, 4, W, W), BF16),
            pltpu.VMEM((C, 4, 4, W, W), BF16),
            pltpu.VMEM((C, 4, 2, 4, H, W), BF16),
            pltpu.VMEM((C, 4, 2, 4, H, W), BF16),
            pltpu.VMEM((C, 4, 4, W, W), BF16),
            pltpu.SMEM((32,), jnp.int32),
            pltpu.SemaphoreType.DMA((NP,)),
            pltpu.SemaphoreType.DMA((C,)),
            pltpu.SemaphoreType.DMA((C, EVENTS)),
            pltpu.SemaphoreType.DMA((C, EVENTS)),
            *[pltpu.VMEM((4, 4, 2, M, W), BF16)] * C,
            *[pltpu.VMEM((4, 4, 2, W, W), BF16)] * C,
        ],
        compiler_params=pltpu.CompilerParams(
            collective_id=1, has_side_effects=True, vmem_limit_bytes=60 << 20),
        cost_estimate=pl.CostEstimate(flops=2 * 32 * M ** 3, bytes_accessed=12 << 20, transcendentals=0),
    )(shifts, sector_dims, psi_blocks[0], left_env[0, 0], right_env[0, 0])
    return out[None]


def solution(mesh):
    in_specs = (
        P("sec", None, None, None),
        P("ops", "sec", None, None),
        P("ops", "sec", None, None),
        P(),
        P(),
    )
    out_specs = P("sec", "ops", None, None)
    return jax.shard_map(body, mesh=mesh, in_specs=in_specs, out_specs=out_specs, check_vma=False)
```

```python
import jax
import jax.numpy as jnp
from jax import lax
from jax.experimental import pallas as pl
from jax.experimental.pallas import tpu as pltpu
from jax.sharding import PartitionSpec as P

MESH = pl.DeviceIdType.MESH
BF16 = jnp.bfloat16
F32 = jnp.float32

M = 512
W = 128
C = M // W
NP = 16
H = W // 2
Q = H // 2
U = 2 * C
NR = NP - 2
HALF = NR // 2

AG0, AG1, AG2, AG3, SIB = 0, 4, 8, 20, 32
GATHER = 38
RS, SWAP, A1, A2, ZOUT = 0, 6, 7, 13, 19
UNIT = 22


class Copy:
    def __init__(self, make):
        self.make = make

    def start(self):
        self.make().start()

    def wait_send(self):
        self.make().wait_send()

    def wait_recv(self):
        self.make().wait_recv()


def start(cs):
    for cp in cs:
        cp.start()


def arrive(cs):
    for cp in cs:
        cp.wait_recv()


def sent(cs):
    for cp in cs:
        cp.wait_send()


def kernel(shifts, dims, psi, left, right, out,
           inter, early, lmask, rmask, rnext, part, part0, rsin, rsin0, sigma, sigma0,
           v, w, x0, x1, zbuf, inv, place_of,
           psem, lsem, osem, gsend, grecv, usend, urecv, *chunked):
    rall, yf = chunked[:C], chunked[C:]
    g = lax.axis_index("ops")
    s = lax.axis_index("sec")
    y, x, c = s // 8, (s // 2) % 4, s % 2

    def dev(dz=0, dy=0, dx=0, dc=0):
        return ((g + dz) % 4, ((y + dy) % 4) * 8 + ((x + dx) % 4) * 2 + (c + dc) % 2)

    def copy(sems, i, e, src, dst, to):
        return Copy(lambda: pltpu.make_async_remote_copy(
            src_ref=src, dst_ref=dst, send_sem=sems[0].at[i, e], recv_sem=sems[1].at[i, e],
            device_id=to, device_id_type=MESH))

    GS, US = (gsend, grecv), (usend, urecv)
    gp, gm, go = (g + 1) % 4, (g + 3) % 4, (g + 2) % 4
    xp, xm, xo = (x + 1) % 4, (x + 3) % 4, (x + 2) % 4
    yp, ym, yo = (y + 1) % 4, (y + 3) % 4, (y + 2) % 4
    XP, XM, YP, YM = dev(dx=1), dev(dx=3), dev(dy=1), dev(dy=3)
    ZP, ZM = dev(dz=1), dev(dz=3)
    SB = dev(dc=1)

    def tile(i, yy, xx, first, count):
        return rall[i].at[yy // 2, yy % 2, xx // 2, xx % 2, c, pl.ds(first, count)]

    def row(i, yy, kind, first, count):
        yh, yl = yy // 2, yy % 2
        if kind == "all":
            return rall[i].at[yh, yl, :, :, c, pl.ds(first, count)]
        return rall[i].at[yh, yl, :, (x + 1) % 2, c, pl.ds(first, count)]

    def col(i, xx, kind, first, count):
        xh, xl = xx // 2, xx % 2
        if kind == "all":
            return rall[i].at[:, :, xh, xl, c, pl.ds(first, count)]
        return rall[i].at[:, (y + 1) % 2, xh, xl, c, pl.ds(first, count)]

    def four(i, e, refs, to):
        return [copy(GS, i, e + k, r, r, d) for k, (r, d) in enumerate(zip(refs, to))]

    def ag0(i):
        a, b = tile(i, y, x, 0, 256), tile(i, y, x, 256, 256)
        return four(i, AG0, (a, a, b, b), (XP, XM, YP, YM))

    def ag1(i):
        return four(i, AG1, (tile(i, y, xm, 0, 128), tile(i, y, xp, 128, 128),
                             tile(i, ym, x, 256, 128), tile(i, yp, x, 384, 128)), (XP, XM, YP, YM))

    def ag2a(i):
        a, b = tile(i, y, x, 0, 256), tile(i, y, x, 256, 256)
        return four(i, AG2, (a, a, b, b), (YP, YM, XP, XM))

    def ag2b(i):
        a, b = row(i, y, "near", 0, 256), col(i, x, "near", 256, 256)
        return four(i, AG2 + 4, (a, a, b, b), (YP, YM, XP, XM))

    def ag2c(i):
        a, b = tile(i, y, xo, 0, 256), tile(i, yo, x, 256, 256)
        return four(i, AG2 + 8, (a, a, b, b), (YP, YM, XP, XM))

    def ag3a(i):
        return four(i, AG3, (tile(i, ym, x, 0, 128), tile(i, yp, x, 128, 128),
                             tile(i, y, xm, 256, 128), tile(i, y, xp, 384, 128)), (YP, YM, XP, XM))

    def ag3b(i):
        return four(i, AG3 + 4, (row(i, ym, "near", 0, 128), row(i, yp, "near", 128, 128),
                                 col(i, xm, "near", 256, 128), col(i, xp, "near", 384, 128)),
                    (YP, YM, XP, XM))

    def ag3c(i):
        return four(i, AG3 + 8, (tile(i, ym, xo, 0, 128), tile(i, yp, xo, 128, 128),
                                 tile(i, yo, xm, 256, 128), tile(i, yo, xp, 384, 128)),
                    (YP, YM, XP, XM))

    def sib(i):
        refs = (row(i, y, "all", 0, 256), col(i, x, "all", 256, 256),
                rall[i].at[:, (y + 1) % 2, :, :, c, pl.ds(0, 256)],
                rall[i].at[:, :, :, (x + 1) % 2, c, pl.ds(256, 256)],
                row(i, yo, "all", 0, 256), col(i, xo, "all", 256, 256))
        return [copy(GS, i, SIB + k, r, r, SB) for k, r in enumerate(refs)]

    def g0(i):
        start(ag0(i) + ag2a(i))

    def g1(i):
        arrive(ag0(i))
        start(ag1(i) + ag2b(i))

    def g2(i):
        arrive(ag1(i))
        start(ag2c(i) + sib(i)[:2])

    def ga(i):
        arrive(ag2a(i) + ag2b(i))
        start(ag3a(i) + ag3b(i))

    def g3(i):
        arrive(ag2c(i))
        start(ag3c(i) + sib(i)[2:4])

    def g4(i):
        arrive(ag3a(i) + ag3b(i) + ag3c(i))
        start(sib(i)[4:])

    def psi_copy(p):
        return pltpu.make_async_copy(psi.at[p], inter.at[p], psem.at[p])

    def lp(i):
        @pl.loop(4 * i, 4 * i + 4)
        def _(p):
            inter[p] = jnp.dot(lmask[...], inter[p], preferred_element_type=F32).astype(BF16)

    def passes(u, send_a, send_b, into, a, b):
        return [copy(US, u, RS, send_a(go), into(0, a), ZM), copy(US, u, RS + 1, send_b(go), into(1, b), ZP),
                copy(US, u, RS + 2, send_a(gp), into(2, a), ZP), copy(US, u, RS + 3, send_b(gm), into(3, b), ZM),
                copy(US, u, RS + 4, send_a(gm), into(4, a), ZM), copy(US, u, RS + 5, send_b(gp), into(5, b), ZP)]

    def rs(u):
        b, r = (u // 2) % 2, pl.ds((u % 2) * H, H)
        return passes(u, lambda d: part.at[b, d, pl.ds(0, HALF), r], lambda d: part.at[b, d, pl.ds(HALF, HALF), r],
                      lambda k, _: rsin.at[u, k], 0, 1)

    def rs0():
        return passes(U, lambda d: part0.at[d, 0], lambda d: part0.at[d, 1], lambda k, _: rsin0.at[k], 0, 1)

    def products(i, first):
        b = i % 2

        @pl.loop(first, first + HALF, unroll=HALF)
        def _(j):
            p = j + (j >= place_of[0]).astype(jnp.int32)
            p = p + (p >= place_of[1]).astype(jnp.int32)
            t = (s + shifts[p]) % 32
            r = jnp.dot(inter[p], rall[i][t // 16, (t // 8) % 2, (t // 4) % 2, (t // 2) % 2, t % 2],
                        preferred_element_type=F32).astype(BF16)
            for d in range(4):
                part[b, d, j] = r[d * W:(d + 1) * W]

    def pr(i):
        arrive(sib(i))
        cs = rs(2 * i)
        products(i, 0)
        start([cs[0], cs[2]])
        products(i, HALF)
        start([cs[1], cs[3]])

    def ps(i):
        start(rs(2 * i + 1)[:4])

    def ad(u):
        b, r = (u // 2) % 2, slice((u % 2) * H, (u % 2) * H + H)
        cs = rs(u)
        for k, d, first in ((0, gm, 0), (1, gp, HALF)):
            cs[k].wait_recv()

            @pl.loop(0, HALF, unroll=HALF)
            def _(j):
                part[b, d, first + j, r] = (part[b, d, first + j, r].astype(F32)
                                            + rsin[u, k, j].astype(F32)).astype(BF16)

            cs[4 + k].start()

    def swap(u):
        return copy(US, u, SWAP, w.at[u], v.at[u, c], SB)

    def fi(u):
        i, r = u // 2, slice((u % 2) * H, (u % 2) * H + H)
        b = i % 2
        cs = rs(u)
        arrive(cs[2:])

        @pl.loop(0, HALF, unroll=HALF)
        def _(j):
            sigma[j] = (part[b, g, j, r].astype(F32) + rsin[u, 2, j].astype(F32)
                        + rsin[u, 4, j].astype(F32)).astype(BF16)
            sigma[j + HALF] = (part[b, g, j + HALF, r].astype(F32) + rsin[u, 3, j].astype(F32)
                               + rsin[u, 5, j].astype(F32)).astype(BF16)

        sigma[NR] = sigma0[0, i, r]
        sigma[NR + 1] = sigma0[1, i, r]

        @pl.loop(0, 16, unroll=4)
        def _(t):
            ty, tx = t // 4, t % 4
            base = ty * 8 + tx * 2 - s + 32
            w[u, ty, tx] = sigma[inv[(base + (c + 1) % 2) % 32]]
            v[u, c, ty, tx] = sigma[inv[(base + c) % 32]]

        swap(u).start()
        sent(cs)

    def next_right():
        return copy(US, U, SWAP, rmask, rnext, SB)

    def s0(_):
        @pl.loop(0, NP)
        def _(p):
            psi_copy(p).wait()

        cs = rs0()
        for k, ref in ((0, rmask), (1, rnext)):
            if k:
                next_right().wait_recv()
            early[...] = jnp.dot(lmask[...], inter[place_of[2 + k]], preferred_element_type=F32).astype(BF16)
            r = jnp.dot(early[...], ref[...], preferred_element_type=F32).astype(BF16)
            for d in range(4):
                for i in range(C):
                    part0[d, k, i] = r[d * W:(d + 1) * W, i * W:(i + 1) * W]
            start([cs[k], cs[2 + k]])

    def s1(_):
        cs = rs0()
        for k, d in ((0, gm), (1, gp)):
            cs[k].wait_recv()
            for i in range(C):
                part0[d, k, i] = (part0[d, k, i].astype(F32) + rsin0[k, i].astype(F32)).astype(BF16)
            cs[4 + k].start()

    def s2(_):
        cs = rs0()
        arrive(cs[2:])
        for k in range(2):
            for i in range(C):
                sigma0[k, i] = (part0[g, k, i].astype(F32) + rsin0[2 + k, i].astype(F32)
                                + rsin0[4 + k, i].astype(F32)).astype(BF16)

    def a1(u):
        cs = []
        for d in (1, 3, 2):
            tx, ty = (x + d) % 4, (y + d) % 4
            cs.append(copy(US, u, A1 + d - 1, v.at[u, :, :, tx, pl.ds(0, Q)], x0.at[u, x], dev(dx=d)))
            cs.append(copy(US, u, A1 + d + 2, v.at[u, :, ty, :, pl.ds(Q, Q)], x1.at[u, y], dev(dy=d)))
        return cs

    def a2(u):
        cs = []
        for d in (1, 3, 2):
            tx, ty = (x + d) % 4, (y + d) % 4
            cs.append(copy(US, u, A2 + d - 1, x0.at[u, :, :, ty], yf[u].at[y, :, :, pl.ds(0, Q)], dev(dy=d)))
            cs.append(copy(US, u, A2 + d + 2, x1.at[u, :, :, tx], yf[u].at[:, x, :, pl.ds(Q, Q)], dev(dx=d)))
        return cs

    def e1(u):
        swap(u).wait_recv()
        start(a1(u))
        for k in range(4):
            for q in range(2):
                x0[u, x, q, k] = v[u, q, k, x, pl.ds(0, Q)]
                x1[u, y, q, k] = v[u, q, y, k, pl.ds(Q, Q)]

    def e2(u):
        arrive(a1(u))
        start(a2(u))
        for k in range(4):
            for q in range(2):
                yf[u][y, k, q, pl.ds(0, Q)] = x0[u, k, q, y]
                yf[u][k, x, q, pl.ds(Q, Q)] = x1[u, k, q, x]

    def place(u):
        return out.at[:, pl.ds(pl.multiple_of(g * W + (u % 2) * H, H), H), pl.ds((u // 2) * W, W)]

    def zout(u):
        return [copy(US, u, ZOUT + d - 1, zbuf.at[u, (g + d) % 4], place(u), dev(dz=d)) for d in (2, 1, 3)]

    def own_out(u):
        return pltpu.make_async_copy(zbuf.at[u, g], place(u), osem.at[u])

    def e3(u):
        arrive(a2(u))

        @pl.loop(0, NP, unroll=4)
        def _(p):
            a = (s - shifts[p] + 32) % 32
            zbuf[u, p // 4, p % 4] = yf[u][a // 8, (a // 2) % 4, a % 2]

        start(zout(u))
        own_out(u).start()

    barrier = pltpu.get_barrier_semaphore()
    peers = ([dev(dz=d) for d in (1, 2, 3)] + [dev(dy=d) for d in (1, 2, 3)]
             + [dev(dx=d) for d in (1, 2, 3)] + [SB])
    for to in peers:
        pl.semaphore_signal(barrier, inc=1, device_id=to, device_id_type=MESH)

    def right_copy(i):
        cols = pl.ds(i * W, W)
        return pltpu.make_async_copy(right.at[:, cols], rmask.at[:, cols], lsem.at[i])

    left_copy = Copy(lambda: pltpu.make_async_copy(left, lmask, lsem.at[C]))
    for i in range(C):
        right_copy(i).start()
    left_copy.start()

    @pl.loop(0, NP)
    def _(p):
        psi_copy(p).start()

    own = dims[s]
    rows = lax.broadcasted_iota(jnp.int32, (M, W), 0)
    cols = lax.broadcasted_iota(jnp.int32, (M, W), 1)

    def masked(ref, i):
        live = (rows < own) & (cols + i * W < own)
        return jnp.where(live, ref[:, i * W:(i + 1) * W].astype(F32), 0.0).astype(BF16)

    def own_right(i):
        right_copy(i).wait()
        r = masked(rmask, i)
        rmask[:, i * W:(i + 1) * W] = r
        rall[i][y // 2, y % 2, x // 2, x % 2, c] = r

    own_right(0)
    pl.semaphore_wait(barrier, len(peers))
    g0(0)
    for i in range(1, C):
        own_right(i)
    next_right().start()
    pltpu.make_async_copy(left, lmask, lsem.at[C]).wait()
    for i in range(C):
        lmask[:, i * W:(i + 1) * W] = masked(lmask, i)

    def slot_of(k):
        r = jnp.int32(0)
        for p in range(NP):
            r = jnp.where(shifts[p] == k, jnp.int32(p), r)
        return r

    pa, pb = slot_of(0), slot_of(1 + 30 * c)
    low, high = jnp.minimum(pa, pb), jnp.maximum(pa, pb)
    place_of[0] = low
    place_of[1] = high
    place_of[2] = pa
    place_of[3] = pb

    @pl.loop(0, 32)
    def _(k):
        p = slot_of(k)
        r = p - (p > low).astype(jnp.int32) - (p > high).astype(jnp.int32)
        r = jnp.where(p == pa, jnp.int32(NR), r)
        inv[k] = jnp.where(p == pb, jnp.int32(NR + 1), r)

    order = (
        (g1, 0), (s0, 0), (g2, 0), (lp, 1), (ga, 0), (lp, 3), (g3, 0), (g0, 1), (s1, 0),
        (lp, 2), (g4, 0), (g1, 1), (lp, 0), (g0, 3), (pr, 0), (s2, 0), (g2, 1), (g0, 2),
        (ga, 1), (ps, 0), (g3, 1), (ad, 0), (g1, 2), (g4, 1), (g2, 2), (ad, 1), (g1, 3),
        (pr, 1), (fi, 0), (ps, 1), (ga, 2), (g3, 2), (g2, 3), (ad, 2), (ga, 3), (g4, 2),
        (e1, 0), (fi, 1), (g3, 3), (ad, 3), (pr, 2), (ps, 2), (fi, 2), (e1, 1), (g4, 3),
        (e2, 0), (fi, 3), (e2, 1), (ad, 4), (pr, 3), (e1, 3), (e1, 2), (ad, 5), (fi, 4),
        (e1, 4), (ps, 3), (e2, 3), (fi, 5), (ad, 6), (e3, 0), (e2, 4), (e1, 5), (ad, 7),
        (e2, 2), (e3, 3), (e2, 5), (fi, 6), (e1, 6), (e3, 1), (fi, 7), (e1, 7), (e3, 5),
        (e3, 4), (e3, 2), (e2, 6), (e2, 7), (e3, 6), (e3, 7),
    )
    for step, i in order:
        step(i)

    for u in range(U):
        arrive(zout(u))
        own_out(u).wait()

    for i in range(C):
        sent(ag0(i) + ag1(i) + ag2a(i) + ag2b(i) + ag2c(i) + ag3a(i) + ag3b(i) + ag3c(i) + sib(i))
    for u in range(U):
        sent([swap(u)] + a1(u) + a2(u) + zout(u))
    sent([next_right()] + rs0())


def body(psi_blocks, left_env, right_env, shifts, sector_dims):
    smem = pl.BlockSpec(memory_space=pltpu.SMEM)
    hbm = pl.BlockSpec(memory_space=pl.ANY)
    out = pl.pallas_call(
        kernel,
        name="sigma",
        out_shape=jax.ShapeDtypeStruct((4, M, M), BF16),
        in_specs=[smem, smem, hbm, hbm, hbm],
        out_specs=hbm,
        scratch_shapes=[
            pltpu.VMEM((NP, M, M), BF16),
            pltpu.VMEM((M, M), BF16),
            pltpu.VMEM((M, M), BF16),
            pltpu.VMEM((M, M), BF16),
            pltpu.VMEM((M, M), BF16),
            pltpu.VMEM((2, 4, NR, W, W), BF16),
            pltpu.VMEM((4, 2, C, W, W), BF16),
            pltpu.VMEM((U, 6, HALF, H, W), BF16),
            pltpu.VMEM((6, C, W, W), BF16),
            pltpu.VMEM((NP, H, W), BF16),
            pltpu.VMEM((2, C, W, W), BF16),
            pltpu.VMEM((U, 2, 4, 4, H, W), BF16),
            pltpu.VMEM((U, 4, 4, H, W), BF16),
            pltpu.VMEM((U, 4, 2, 4, Q, W), BF16),
            pltpu.VMEM((U, 4, 2, 4, Q, W), BF16),
            pltpu.VMEM((U, 4, 4, H, W), BF16),
            pltpu.SMEM((32,), jnp.int32),
            pltpu.SMEM((4,), jnp.int32),
            pltpu.SemaphoreType.DMA((NP,)),
            pltpu.SemaphoreType.DMA((C + 1,)),
            pltpu.SemaphoreType.DMA((U,)),
            pltpu.SemaphoreType.DMA((C, GATHER)),
            pltpu.SemaphoreType.DMA((C, GATHER)),
            pltpu.SemaphoreType.DMA((U + 1, UNIT)),
            pltpu.SemaphoreType.DMA((U + 1, UNIT)),
            *[pltpu.VMEM((2, 2, 2, 2, 2, M, W), BF16)] * C,
            *[pltpu.VMEM((4, 4, 2, H, W), BF16)] * U,
        ],
        compiler_params=pltpu.CompilerParams(
            collective_id=1, has_side_effects=True, vmem_limit_bytes=60 << 20),
        cost_estimate=pl.CostEstimate(flops=2 * 32 * M ** 3, bytes_accessed=12 << 20, transcendentals=0),
    )(shifts, sector_dims, psi_blocks[0], left_env[0, 0], right_env[0, 0])
    return out[None]


def solution(mesh):
    in_specs = (
        P("sec", None, None, None),
        P("ops", "sec", None, None),
        P("ops", "sec", None, None),
        P(),
        P(),
    )
    out_specs = P("sec", "ops", None, None)
    return jax.shard_map(body, mesh=mesh, in_specs=in_specs, out_specs=out_specs, check_vma=False)
```

```python
import jax
import jax.numpy as jnp
from jax import lax
from jax.experimental import pallas as pl
from jax.experimental.pallas import tpu as pltpu
from jax.sharding import PartitionSpec as P

MESH = pl.DeviceIdType.MESH
BF16 = jnp.bfloat16
F32 = jnp.float32

M = 512
W = 128
C = M // W
NP = 16
H = W // 2
Q = H // 2
U = 2 * C
NR = NP - 2
HALF = NR // 2

AG0, AG1, AG2, AG2C, AG3, SIB = range(6)
GATHER = 6
RS, RSB, RSC, SWAP, A1, A2, ZOUT = range(7)
UNIT = 7


class Copy:
    def __init__(self, make):
        self.make = make

    def start(self):
        self.make().start()

    def wait_recv(self):
        self.make().wait_recv()


def start(cs):
    for cp in cs:
        cp.start()


def kernel(shifts, dims, psi, left, right, out,
           inter, early, lmask, rmask, rnext, part, part0, rsin, rsin0, sigma, sigma0,
           v, w, x0, x1, zbuf, inv, place_of,
           psem, lsem, osem, gsend, grecv, rsend, xsend, urecv, *chunked):
    rall, yf = chunked[:C], chunked[C:]
    g = lax.axis_index("ops")
    s = lax.axis_index("sec")
    y, x, c = s // 8, (s // 2) % 4, s % 2

    def dev(dz=0, dy=0, dx=0, dc=0):
        return ((g + dz) % 4, ((y + dy) % 4) * 8 + ((x + dx) % 4) * 2 + (c + dc) % 2)

    SB = dev(dc=1)

    def copy(send, recv, src, dst, to):
        return Copy(lambda: pltpu.make_async_remote_copy(
            src_ref=src, dst_ref=dst, send_sem=send, recv_sem=recv, device_id=to, device_id_type=MESH))

    def take(sem, kib, received=True):
        n = next(n for n in range(1, NP + 1) if kib <= n * M and kib % (16 * n) == 0)
        view = inter.at[pl.ds(0, n), pl.ds(0, kib // n)]
        cp = pltpu.make_async_remote_copy(
            src_ref=view, dst_ref=view, send_sem=sem, recv_sem=sem, device_id=SB, device_id_type=MESH)
        if received:
            cp.wait_recv()
        else:
            cp.wait_send()

    gp, gm, go = (g + 1) % 4, (g + 3) % 4, (g + 2) % 4
    xp, xm, xo = (x + 1) % 4, (x + 3) % 4, (x + 2) % 4
    yp, ym, yo = (y + 1) % 4, (y + 3) % 4, (y + 2) % 4
    XP, XM, YP, YM = dev(dx=1), dev(dx=3), dev(dy=1), dev(dy=3)
    ZP, ZM = dev(dz=1), dev(dz=3)

    def tile(i, yy, xx, first, count):
        return rall[i].at[yy // 2, yy % 2, xx // 2, xx % 2, c, pl.ds(first, count)]

    def row(i, yy, kind, first, count):
        yh, yl = yy // 2, yy % 2
        if kind == "all":
            return rall[i].at[yh, yl, :, :, c, pl.ds(first, count)]
        return rall[i].at[yh, yl, :, (x + 1) % 2, c, pl.ds(first, count)]

    def col(i, xx, kind, first, count):
        xh, xl = xx // 2, xx % 2
        if kind == "all":
            return rall[i].at[:, :, xh, xl, c, pl.ds(first, count)]
        return rall[i].at[:, (y + 1) % 2, xh, xl, c, pl.ds(first, count)]

    def four(i, e, refs, to):
        return [copy(gsend.at[i], grecv.at[i, e], r, r, d) for r, d in zip(refs, to)]

    def ag0(i):
        a, b = tile(i, y, x, 0, 256), tile(i, y, x, 256, 256)
        return four(i, AG0, (a, a, b, b), (XP, XM, YP, YM))

    def ag1(i):
        return four(i, AG1, (tile(i, y, xm, 0, 128), tile(i, y, xp, 128, 128),
                             tile(i, ym, x, 256, 128), tile(i, yp, x, 384, 128)), (XP, XM, YP, YM))

    def ag2a(i):
        a, b = tile(i, y, x, 0, 256), tile(i, y, x, 256, 256)
        return four(i, AG2, (a, a, b, b), (YP, YM, XP, XM))

    def ag2b(i):
        a, b = row(i, y, "near", 0, 256), col(i, x, "near", 256, 256)
        return four(i, AG2, (a, a, b, b), (YP, YM, XP, XM))

    def ag2c(i):
        a, b = tile(i, y, xo, 0, 256), tile(i, yo, x, 256, 256)
        return four(i, AG2C, (a, a, b, b), (YP, YM, XP, XM))

    def ag3a(i):
        return four(i, AG3, (tile(i, ym, x, 0, 128), tile(i, yp, x, 128, 128),
                             tile(i, y, xm, 256, 128), tile(i, y, xp, 384, 128)), (YP, YM, XP, XM))

    def ag3b(i):
        return four(i, AG3, (row(i, ym, "near", 0, 128), row(i, yp, "near", 128, 128),
                                 col(i, xm, "near", 256, 128), col(i, xp, "near", 384, 128)),
                    (YP, YM, XP, XM))

    def ag3c(i):
        return four(i, AG3, (tile(i, ym, xo, 0, 128), tile(i, yp, xo, 128, 128),
                                 tile(i, yo, xm, 256, 128), tile(i, yo, xp, 384, 128)),
                    (YP, YM, XP, XM))

    def sib(i):
        refs = (row(i, y, "all", 0, 256), col(i, x, "all", 256, 256),
                rall[i].at[:, (y + 1) % 2, :, :, c, pl.ds(0, 256)],
                rall[i].at[:, :, :, (x + 1) % 2, c, pl.ds(256, 256)],
                row(i, yo, "all", 0, 256), col(i, xo, "all", 256, 256))
        return [copy(gsend.at[i], grecv.at[i, SIB], r, r, SB) for r in refs]

    def g0(i):
        start(ag0(i) + ag2a(i))

    def g1(i):
        take(grecv.at[i, AG0], 256)
        start(ag1(i) + ag2b(i))

    def g2(i):
        take(grecv.at[i, AG1], 128)
        start(ag2c(i) + sib(i)[:2])

    def ga(i):
        take(grecv.at[i, AG2], 768)
        start(ag3a(i) + ag3b(i))

    def g3(i):
        take(grecv.at[i, AG2C], 256)
        start(ag3c(i) + sib(i)[2:4])

    def g4(i):
        take(grecv.at[i, AG3], 512)
        start(sib(i)[4:])

    def psi_copy(k):
        four_blocks = pl.ds(4 * k, 4)
        return pltpu.make_async_copy(psi.at[four_blocks], inter.at[four_blocks], psem.at[k])

    def lp(i):
        @pl.loop(4 * i, 4 * i + 4)
        def _(p):
            inter[p] = jnp.dot(lmask[...], inter[p], preferred_element_type=F32).astype(BF16)

    def passes(u, send_a, send_b, into):
        def to(e, k, src, device):
            return copy(rsend.at[u], urecv.at[u, e], src, into(k), device)

        return [to(RS, 0, send_a(go), ZM), to(RSB, 1, send_b(go), ZP),
                to(RSC, 2, send_a(gp), ZP), to(RSC, 3, send_b(gm), ZM),
                to(RSC, 4, send_a(gm), ZM), to(RSC, 5, send_b(gp), ZP)]

    def rs(u):
        b, r = (u // 2) % 2, pl.ds((u % 2) * H, H)
        return passes(u, lambda d: part.at[b, d, pl.ds(0, HALF), r], lambda d: part.at[b, d, pl.ds(HALF, HALF), r],
                      lambda k: rsin.at[u, k])

    def rs0():
        return passes(U, lambda d: part0.at[d, 0], lambda d: part0.at[d, 1], lambda k: rsin0.at[k])

    def products(i, first):
        b = i % 2

        @pl.loop(first, first + HALF, unroll=HALF)
        def _(j):
            p = j + (j >= place_of[0]).astype(jnp.int32)
            p = p + (p >= place_of[1]).astype(jnp.int32)
            t = (s + shifts[p]) % 32
            r = jnp.dot(inter[p], rall[i][t // 16, (t // 8) % 2, (t // 4) % 2, (t // 2) % 2, t % 2],
                        preferred_element_type=F32).astype(BF16)
            for d in range(4):
                part[b, d, j] = r[d * W:(d + 1) * W]

    def pr(i):
        take(grecv.at[i, SIB], 2048)
        cs = rs(2 * i)
        products(i, 0)
        start([cs[0], cs[2]])
        products(i, HALF)
        start([cs[1], cs[3]])

    def ps(i):
        start(rs(2 * i + 1)[:4])

    def ad(u):
        b, r = (u // 2) % 2, slice((u % 2) * H, (u % 2) * H + H)
        cs = rs(u)
        for k, d, first in ((0, gm, 0), (1, gp, HALF)):
            cs[k].wait_recv()

            @pl.loop(0, HALF, unroll=HALF)
            def _(j):
                part[b, d, first + j, r] = (part[b, d, first + j, r].astype(F32)
                                            + rsin[u, k, j].astype(F32)).astype(BF16)

            cs[4 + k].start()

    def swap(u):
        return copy(xsend.at[u // 4], urecv.at[u, SWAP], w.at[u], v.at[u, c], SB)

    def fi(u):
        i, r = u // 2, slice((u % 2) * H, (u % 2) * H + H)
        b = i % 2
        take(urecv.at[u, RSC], 448)

        @pl.loop(0, HALF, unroll=HALF)
        def _(j):
            sigma[j] = (part[b, g, j, r].astype(F32) + rsin[u, 2, j].astype(F32)
                        + rsin[u, 4, j].astype(F32)).astype(BF16)
            sigma[j + HALF] = (part[b, g, j + HALF, r].astype(F32) + rsin[u, 3, j].astype(F32)
                               + rsin[u, 5, j].astype(F32)).astype(BF16)

        sigma[NR] = sigma0[0, i, r]
        sigma[NR + 1] = sigma0[1, i, r]

        @pl.loop(0, 16, unroll=4)
        def _(t):
            ty, tx = t // 4, t % 4
            base = ty * 8 + tx * 2 - s + 32
            w[u, ty, tx] = sigma[inv[(base + (c + 1) % 2) % 32]]
            v[u, c, ty, tx] = sigma[inv[(base + c) % 32]]

        swap(u).start()
        take(rsend.at[u], 672, False)

    def next_right():
        return copy(xsend.at[2], urecv.at[U, SWAP], rmask, rnext, SB)

    def s0(_):
        for k in range(4):
            psi_copy(k).wait()

        cs = rs0()
        for k, ref in ((0, rmask), (1, rnext)):
            if k:
                next_right().wait_recv()
            early[...] = jnp.dot(lmask[...], inter[place_of[2 + k]], preferred_element_type=F32).astype(BF16)
            r = jnp.dot(early[...], ref[...], preferred_element_type=F32).astype(BF16)
            for d in range(4):
                for i in range(C):
                    part0[d, k, i] = r[d * W:(d + 1) * W, i * W:(i + 1) * W]
            start([cs[k], cs[2 + k]])

    def s1(_):
        cs = rs0()
        for k, d in ((0, gm), (1, gp)):
            cs[k].wait_recv()
            for i in range(C):
                part0[d, k, i] = (part0[d, k, i].astype(F32) + rsin0[k, i].astype(F32)).astype(BF16)
            cs[4 + k].start()

    def s2(_):
        take(urecv.at[U, RSC], 512)
        for k in range(2):
            for i in range(C):
                sigma0[k, i] = (part0[g, k, i].astype(F32) + rsin0[2 + k, i].astype(F32)
                                + rsin0[4 + k, i].astype(F32)).astype(BF16)

    def a1(u):
        cs = []
        for d in (1, 3, 2):
            tx, ty = (x + d) % 4, (y + d) % 4
            cs.append(copy(xsend.at[u // 4], urecv.at[u, A1], v.at[u, :, :, tx, pl.ds(0, Q)], x0.at[u, x], dev(dx=d)))
            cs.append(copy(xsend.at[u // 4], urecv.at[u, A1], v.at[u, :, ty, :, pl.ds(Q, Q)], x1.at[u, y], dev(dy=d)))
        return cs

    def a2(u):
        cs = []
        for d in (1, 3, 2):
            tx, ty = (x + d) % 4, (y + d) % 4
            cs.append(copy(xsend.at[u // 4], urecv.at[u, A2], x0.at[u, :, :, ty], yf[u].at[y, :, :, pl.ds(0, Q)], dev(dy=d)))
            cs.append(copy(xsend.at[u // 4], urecv.at[u, A2], x1.at[u, :, :, tx], yf[u].at[:, x, :, pl.ds(Q, Q)], dev(dx=d)))
        return cs

    def e1(u):
        swap(u).wait_recv()
        start(a1(u))
        for k in range(4):
            for q in range(2):
                x0[u, x, q, k] = v[u, q, k, x, pl.ds(0, Q)]
                x1[u, y, q, k] = v[u, q, y, k, pl.ds(Q, Q)]

    def e2(u):
        take(urecv.at[u, A1], 384)
        start(a2(u))
        for k in range(4):
            for q in range(2):
                yf[u][y, k, q, pl.ds(0, Q)] = x0[u, k, q, y]
                yf[u][k, x, q, pl.ds(Q, Q)] = x1[u, k, q, x]

    def place(u):
        return out.at[:, pl.ds(pl.multiple_of(g * W + (u % 2) * H, H), H), pl.ds((u // 2) * W, W)]

    def zout(u):
        return [copy(xsend.at[u // 4], urecv.at[u, ZOUT], zbuf.at[u, (g + d) % 4], place(u), dev(dz=d)) for d in (2, 1, 3)]

    def own_out(u):
        return pltpu.make_async_copy(zbuf.at[u, g], place(u), osem.at[u])

    def e3(u):
        take(urecv.at[u, A2], 384)

        @pl.loop(0, NP, unroll=4)
        def _(p):
            a = (s - shifts[p] + 32) % 32
            zbuf[u, p // 4, p % 4] = yf[u][a // 8, (a // 2) % 4, a % 2]

        start(zout(u))
        own_out(u).start()

    barrier = pltpu.get_barrier_semaphore()
    peers = ([dev(dz=d) for d in (1, 2, 3)] + [dev(dy=d) for d in (1, 2, 3)]
             + [dev(dx=d) for d in (1, 2, 3)] + [SB])
    for to in peers:
        pl.semaphore_signal(barrier, inc=1, device_id=to, device_id_type=MESH)

    def right_copy(i):
        cols = pl.ds(i * W, W)
        return pltpu.make_async_copy(right.at[:, cols], rmask.at[:, cols], lsem.at[i])

    left_copy = Copy(lambda: pltpu.make_async_copy(left, lmask, lsem.at[C]))
    for i in range(C):
        right_copy(i).start()
    left_copy.start()

    for k in range(4):
        psi_copy(k).start()

    own = dims[s]
    rows = lax.broadcasted_iota(jnp.int32, (M, W), 0)
    cols = lax.broadcasted_iota(jnp.int32, (M, W), 1)

    def masked(ref, i):
        live = (rows < own) & (cols + i * W < own)
        return jnp.where(live, ref[:, i * W:(i + 1) * W].astype(F32), 0.0).astype(BF16)

    def own_right(i):
        right_copy(i).wait()
        r = masked(rmask, i)
        rmask[:, i * W:(i + 1) * W] = r
        rall[i][y // 2, y % 2, x // 2, x % 2, c] = r

    own_right(0)
    pl.semaphore_wait(barrier, len(peers))
    g0(0)
    for i in range(1, C):
        own_right(i)
    next_right().start()
    pltpu.make_async_copy(left, lmask, lsem.at[C]).wait()
    for i in range(C):
        lmask[:, i * W:(i + 1) * W] = masked(lmask, i)

    def slot_of(k):
        r = jnp.int32(0)
        for p in range(NP):
            r = jnp.where(shifts[p] == k, jnp.int32(p), r)
        return r

    pa, pb = slot_of(0), slot_of(1 + 30 * c)
    low, high = jnp.minimum(pa, pb), jnp.maximum(pa, pb)
    place_of[0] = low
    place_of[1] = high
    place_of[2] = pa
    place_of[3] = pb

    @pl.loop(0, 32)
    def _(k):
        p = slot_of(k)
        r = p - (p > low).astype(jnp.int32) - (p > high).astype(jnp.int32)
        r = jnp.where(p == pa, jnp.int32(NR), r)
        inv[k] = jnp.where(p == pb, jnp.int32(NR + 1), r)

    order = (
        (g1, 0), (s0, 0), (g2, 0), (lp, 1), (ga, 0), (lp, 3), (g3, 0), (g0, 1), (s1, 0),
        (lp, 2), (g4, 0), (g1, 1), (lp, 0), (g0, 3), (pr, 0), (s2, 0), (g2, 1), (g0, 2),
        (ga, 1), (ps, 0), (g3, 1), (ad, 0), (g1, 2), (g4, 1), (g2, 2), (ad, 1), (g1, 3),
        (pr, 1), (fi, 0), (ps, 1), (ga, 2), (g3, 2), (g2, 3), (ad, 2), (ga, 3), (g4, 2),
        (e1, 0), (fi, 1), (g3, 3), (ad, 3), (pr, 2), (ps, 2), (fi, 2), (e1, 1), (g4, 3),
        (e2, 0), (fi, 3), (e2, 1), (ad, 4), (pr, 3), (e1, 3), (e1, 2), (ad, 5), (fi, 4),
        (e1, 4), (ps, 3), (e2, 3), (fi, 5), (ad, 6), (e3, 0), (e2, 4), (e1, 5), (ad, 7),
        (e2, 2), (e3, 3), (e2, 5), (fi, 6), (e1, 6), (e3, 1), (fi, 7), (e1, 7), (e3, 5),
        (e3, 4), (e3, 2), (e2, 6), (e2, 7), (e3, 6), (e3, 7),
    )
    for step, i in order:
        step(i)

    for u in range(U):
        take(urecv.at[u, ZOUT], 192)
        own_out(u).wait()
    for i in range(C):
        take(gsend.at[i], 3968, False)
    for k in range(2):
        take(xsend.at[k], 4864, False)
    take(xsend.at[2], 512, False)
    take(rsend.at[U], 768, False)


def body(psi_blocks, left_env, right_env, shifts, sector_dims):
    smem = pl.BlockSpec(memory_space=pltpu.SMEM)
    hbm = pl.BlockSpec(memory_space=pl.ANY)
    out = pl.pallas_call(
        kernel,
        name="sigma",
        out_shape=jax.ShapeDtypeStruct((4, M, M), BF16),
        in_specs=[smem, smem, hbm, hbm, hbm],
        out_specs=hbm,
        scratch_shapes=[
            pltpu.VMEM((NP, M, M), BF16),
            pltpu.VMEM((M, M), BF16),
            pltpu.VMEM((M, M), BF16),
            pltpu.VMEM((M, M), BF16),
            pltpu.VMEM((M, M), BF16),
            pltpu.VMEM((2, 4, NR, W, W), BF16),
            pltpu.VMEM((4, 2, C, W, W), BF16),
            pltpu.VMEM((U, 6, HALF, H, W), BF16),
            pltpu.VMEM((6, C, W, W), BF16),
            pltpu.VMEM((NP, H, W), BF16),
            pltpu.VMEM((2, C, W, W), BF16),
            pltpu.VMEM((U, 2, 4, 4, H, W), BF16),
            pltpu.VMEM((U, 4, 4, H, W), BF16),
            pltpu.VMEM((U, 4, 2, 4, Q, W), BF16),
            pltpu.VMEM((U, 4, 2, 4, Q, W), BF16),
            pltpu.VMEM((U, 4, 4, H, W), BF16),
            pltpu.SMEM((32,), jnp.int32),
            pltpu.SMEM((4,), jnp.int32),
            pltpu.SemaphoreType.DMA((4,)),
            pltpu.SemaphoreType.DMA((C + 1,)),
            pltpu.SemaphoreType.DMA((U,)),
            pltpu.SemaphoreType.DMA((C,)),
            pltpu.SemaphoreType.DMA((C, GATHER)),
            pltpu.SemaphoreType.DMA((U + 1,)),
            pltpu.SemaphoreType.DMA((3,)),
            pltpu.SemaphoreType.DMA((U + 1, UNIT)),
            *[pltpu.VMEM((2, 2, 2, 2, 2, M, W), BF16)] * C,
            *[pltpu.VMEM((4, 4, 2, H, W), BF16)] * U,
        ],
        compiler_params=pltpu.CompilerParams(
            collective_id=1, has_side_effects=True, vmem_limit_bytes=60 << 20),
        cost_estimate=pl.CostEstimate(flops=2 * 32 * M ** 3, bytes_accessed=12 << 20, transcendentals=0),
    )(shifts, sector_dims, psi_blocks[0], left_env[0, 0], right_env[0, 0])
    return out[None]


def solution(mesh):
    in_specs = (
        P("sec", None, None, None),
        P("ops", "sec", None, None),
        P("ops", "sec", None, None),
        P(),
        P(),
    )
    out_specs = P("sec", "ops", None, None)
    return jax.shard_map(body, mesh=mesh, in_specs=in_specs, out_specs=out_specs, check_vma=False)
```

```python
import jax
import jax.numpy as jnp
from jax import lax
from jax.experimental import pallas as pl
from jax.experimental.pallas import tpu as pltpu
from jax.sharding import PartitionSpec as P

MESH = pl.DeviceIdType.MESH
BF16 = jnp.bfloat16
F32 = jnp.float32

M = 512
W = 128
C = M // W
NP = 16
H = W // 2
Q = H // 2
U = 2 * C
NR = NP - 2
HALF = NR // 2

AG0, AG1, AG2, AG2C, AG3, SIB = range(6)
GATHER = 6
RS, RSB, RSC, SWAP, A1, A2, ZOUT = range(7)
UNIT = 7


class Copy:
    def __init__(self, make):
        self.make = make

    def start(self):
        self.make().start()

    def wait_recv(self):
        self.make().wait_recv()


def start(cs):
    for cp in cs:
        cp.start()


def kernel(shifts, dims, psi, left, right, out,
           inter, early, lmask, rmask, rnext, part, part0, rsin, rsin0, sigma, sigma0,
           v, w, x0, x1, zbuf, inv, place_of,
           psem, lsem, osem, gsend, grecv, rsend, xsend, urecv, *chunked):
    rall, yf = chunked[:C], chunked[C:]
    g = lax.axis_index("ops")
    s = lax.axis_index("sec")
    y, x, c = s // 8, (s // 2) % 4, s % 2

    def dev(dz=0, dy=0, dx=0, dc=0):
        return ((g + dz) % 4, ((y + dy) % 4) * 8 + ((x + dx) % 4) * 2 + (c + dc) % 2)

    SB = dev(dc=1)

    def copy(send, recv, src, dst, to):
        return Copy(lambda: pltpu.make_async_remote_copy(
            src_ref=src, dst_ref=dst, send_sem=send, recv_sem=recv, device_id=to, device_id_type=MESH))

    def take(sem, kib, received=True):
        n = next(n for n in range(1, NP + 1) if kib <= n * M and kib % (16 * n) == 0)
        view = inter.at[pl.ds(0, n), pl.ds(0, kib // n)]
        cp = pltpu.make_async_remote_copy(
            src_ref=view, dst_ref=view, send_sem=sem, recv_sem=sem, device_id=SB, device_id_type=MESH)
        if received:
            cp.wait_recv()
        else:
            cp.wait_send()

    gp, gm, go = (g + 1) % 4, (g + 3) % 4, (g + 2) % 4
    xp, xm, xo = (x + 1) % 4, (x + 3) % 4, (x + 2) % 4
    yp, ym, yo = (y + 1) % 4, (y + 3) % 4, (y + 2) % 4
    XP, XM, YP, YM = dev(dx=1), dev(dx=3), dev(dy=1), dev(dy=3)
    ZP, ZM = dev(dz=1), dev(dz=3)

    def tile(i, yy, xx, first, count):
        return rall[i].at[yy // 2, yy % 2, xx // 2, xx % 2, c, pl.ds(first, count)]

    def row(i, yy, kind, first, count):
        yh, yl = yy // 2, yy % 2
        if kind == "all":
            return rall[i].at[yh, yl, :, :, c, pl.ds(first, count)]
        return rall[i].at[yh, yl, :, (x + 1) % 2, c, pl.ds(first, count)]

    def col(i, xx, kind, first, count):
        xh, xl = xx // 2, xx % 2
        if kind == "all":
            return rall[i].at[:, :, xh, xl, c, pl.ds(first, count)]
        return rall[i].at[:, (y + 1) % 2, xh, xl, c, pl.ds(first, count)]

    def four(i, e, refs, to):
        return [copy(gsend.at[i], grecv.at[i, e], r, r, d) for r, d in zip(refs, to)]

    def ag0(i):
        a, b = tile(i, y, x, 0, 256), tile(i, y, x, 256, 256)
        return four(i, AG0, (a, a, b, b), (XP, XM, YP, YM))

    def ag1(i):
        return four(i, AG1, (tile(i, y, xm, 0, 128), tile(i, y, xp, 128, 128),
                             tile(i, ym, x, 256, 128), tile(i, yp, x, 384, 128)), (XP, XM, YP, YM))

    def ag2a(i):
        a, b = tile(i, y, x, 0, 256), tile(i, y, x, 256, 256)
        return four(i, AG2, (a, a, b, b), (YP, YM, XP, XM))

    def ag2b(i):
        a, b = row(i, y, "near", 0, 256), col(i, x, "near", 256, 256)
        return four(i, AG2, (a, a, b, b), (YP, YM, XP, XM))

    def ag2c(i):
        a, b = tile(i, y, xo, 0, 256), tile(i, yo, x, 256, 256)
        return four(i, AG2C, (a, a, b, b), (YP, YM, XP, XM))

    def ag3a(i):
        return four(i, AG3, (tile(i, ym, x, 0, 128), tile(i, yp, x, 128, 128),
                             tile(i, y, xm, 256, 128), tile(i, y, xp, 384, 128)), (YP, YM, XP, XM))

    def ag3b(i):
        return four(i, AG3, (row(i, ym, "near", 0, 128), row(i, yp, "near", 128, 128),
                                 col(i, xm, "near", 256, 128), col(i, xp, "near", 384, 128)),
                    (YP, YM, XP, XM))

    def ag3c(i):
        return four(i, AG3, (tile(i, ym, xo, 0, 128), tile(i, yp, xo, 128, 128),
                                 tile(i, yo, xm, 256, 128), tile(i, yo, xp, 384, 128)),
                    (YP, YM, XP, XM))

    def sib(i):
        refs = (row(i, y, "all", 0, 256), col(i, x, "all", 256, 256),
                rall[i].at[:, (y + 1) % 2, :, :, c, pl.ds(0, 256)],
                rall[i].at[:, :, :, (x + 1) % 2, c, pl.ds(256, 256)],
                row(i, yo, "all", 0, 256), col(i, xo, "all", 256, 256))
        return [copy(gsend.at[i], grecv.at[i, SIB], r, r, SB) for r in refs]

    def g0(i):
        start(ag0(i) + ag2a(i))

    def g1(i):
        take(grecv.at[i, AG0], 256)
        start(ag1(i) + ag2b(i))

    def g2(i):
        take(grecv.at[i, AG1], 128)
        start(ag2c(i) + sib(i)[:2])

    def ga(i):
        take(grecv.at[i, AG2], 768)
        start(ag3a(i) + ag3b(i))

    def g3(i):
        take(grecv.at[i, AG2C], 256)
        start(ag3c(i) + sib(i)[2:4])

    def g4(i):
        take(grecv.at[i, AG3], 512)
        start(sib(i)[4:])

    def psi_copy(k):
        four_blocks = pl.ds(4 * k, 4)
        return pltpu.make_async_copy(psi.at[four_blocks], inter.at[four_blocks], psem.at[k])

    def lp(i):
        @pl.loop(4 * i, 4 * i + 4)
        def _(p):
            inter[p] = jnp.dot(lmask[...], inter[p], preferred_element_type=F32).astype(BF16)

    def passes(u, send_a, send_b, into):
        def to(e, k, src, device):
            return copy(rsend.at[u], urecv.at[u, e], src, into(k), device)

        return [to(RS, 0, send_a(go), ZM), to(RSB, 1, send_b(go), ZP),
                to(RSC, 2, send_a(gp), ZP), to(RSC, 3, send_b(gm), ZM),
                to(RSC, 4, send_a(gm), ZM), to(RSC, 5, send_b(gp), ZP)]

    def rs(u):
        b, r = (u // 2) % 2, pl.ds((u % 2) * H, H)
        return passes(u, lambda d: part.at[b, d, pl.ds(0, HALF), r], lambda d: part.at[b, d, pl.ds(HALF, HALF), r],
                      lambda k: rsin.at[u, k])

    def rs0():
        return passes(U, lambda d: part0.at[d, 0], lambda d: part0.at[d, 1], lambda k: rsin0.at[k])

    def products(i, first):
        b = i % 2

        @pl.loop(first, first + HALF, unroll=HALF)
        def _(j):
            p = j + (j >= place_of[0]).astype(jnp.int32)
            p = p + (p >= place_of[1]).astype(jnp.int32)
            t = (s + shifts[p]) % 32
            r = jnp.dot(inter[p], rall[i][t // 16, (t // 8) % 2, (t // 4) % 2, (t // 2) % 2, t % 2],
                        preferred_element_type=F32).astype(BF16)
            for d in range(4):
                part[b, d, j] = r[d * W:(d + 1) * W]

    def pr(i):
        take(grecv.at[i, SIB], 2048)
        cs = rs(2 * i)
        products(i, 0)
        start([cs[0], cs[2]])
        products(i, HALF)
        start([cs[1], cs[3]])

    def ps(i):
        start(rs(2 * i + 1)[:4])

    def ad(u):
        b, r = (u // 2) % 2, slice((u % 2) * H, (u % 2) * H + H)
        cs = rs(u)
        for k, d, first in ((0, gm, 0), (1, gp, HALF)):
            cs[k].wait_recv()

            @pl.loop(0, HALF, unroll=HALF)
            def _(j):
                part[b, d, first + j, r] = (part[b, d, first + j, r].astype(F32)
                                            + rsin[u, k, j].astype(F32)).astype(BF16)

            cs[4 + k].start()

    def swap(u):
        return copy(xsend.at[u // 4], urecv.at[u, SWAP], w.at[u], v.at[u, c], SB)

    def fi(u):
        i, r = u // 2, slice((u % 2) * H, (u % 2) * H + H)
        b = i % 2
        take(urecv.at[u, RSC], 448)

        @pl.loop(0, HALF, unroll=HALF)
        def _(j):
            sigma[j] = (part[b, g, j, r].astype(F32) + rsin[u, 2, j].astype(F32)
                        + rsin[u, 4, j].astype(F32)).astype(BF16)
            sigma[j + HALF] = (part[b, g, j + HALF, r].astype(F32) + rsin[u, 3, j].astype(F32)
                               + rsin[u, 5, j].astype(F32)).astype(BF16)

        sigma[NR] = sigma0[0, i, r]
        sigma[NR + 1] = sigma0[1, i, r]

        @pl.loop(0, 16, unroll=4)
        def _(t):
            ty, tx = t // 4, t % 4
            base = ty * 8 + tx * 2 - s + 32
            w[u, ty, tx] = sigma[inv[(base + (c + 1) % 2) % 32]]
            v[u, c, ty, tx] = sigma[inv[(base + c) % 32]]

        swap(u).start()
        take(rsend.at[u], 672, False)

    def next_right():
        return copy(xsend.at[2], urecv.at[U, SWAP], rmask, rnext, SB)

    def s0(_):
        for k in range(4):
            psi_copy(k).wait()

        cs = rs0()
        for k, ref in ((0, rmask), (1, rnext)):
            if k:
                next_right().wait_recv()
            early[...] = jnp.dot(lmask[...], inter[place_of[2 + k]], preferred_element_type=F32).astype(BF16)
            r = jnp.dot(early[...], ref[...], preferred_element_type=F32).astype(BF16)
            for d in range(4):
                for i in range(C):
                    part0[d, k, i] = r[d * W:(d + 1) * W, i * W:(i + 1) * W]
            start([cs[k], cs[2 + k]])

    def s1(_):
        cs = rs0()
        for k, d in ((0, gm), (1, gp)):
            cs[k].wait_recv()
            for i in range(C):
                part0[d, k, i] = (part0[d, k, i].astype(F32) + rsin0[k, i].astype(F32)).astype(BF16)
            cs[4 + k].start()

    def s2(_):
        take(urecv.at[U, RSC], 512)
        for k in range(2):
            for i in range(C):
                sigma0[k, i] = (part0[g, k, i].astype(F32) + rsin0[2 + k, i].astype(F32)
                                + rsin0[4 + k, i].astype(F32)).astype(BF16)

    def a1(u):
        cs = []
        for d in (1, 3, 2):
            tx, ty = (x + d) % 4, (y + d) % 4
            cs.append(copy(xsend.at[u // 4], urecv.at[u, A1], v.at[u, :, :, tx, pl.ds(0, Q)], x0.at[u, x], dev(dx=d)))
            cs.append(copy(xsend.at[u // 4], urecv.at[u, A1], v.at[u, :, ty, :, pl.ds(Q, Q)], x1.at[u, y], dev(dy=d)))
        return cs

    def a2(u):
        cs = []
        for d in (1, 3, 2):
            tx, ty = (x + d) % 4, (y + d) % 4
            cs.append(copy(xsend.at[u // 4], urecv.at[u, A2], x0.at[u, :, :, ty], yf[u].at[y, :, :, pl.ds(0, Q)], dev(dy=d)))
            cs.append(copy(xsend.at[u // 4], urecv.at[u, A2], x1.at[u, :, :, tx], yf[u].at[:, x, :, pl.ds(Q, Q)], dev(dx=d)))
        return cs

    def e1(u):
        swap(u).wait_recv()
        start(a1(u))
        for k in range(4):
            for q in range(2):
                x0[u, x, q, k] = v[u, q, k, x, pl.ds(0, Q)]
                x1[u, y, q, k] = v[u, q, y, k, pl.ds(Q, Q)]

    def e2(u):
        take(urecv.at[u, A1], 384)
        start(a2(u))
        for k in range(4):
            for q in range(2):
                yf[u][y, k, q, pl.ds(0, Q)] = x0[u, k, q, y]
                yf[u][k, x, q, pl.ds(Q, Q)] = x1[u, k, q, x]

    def place(u):
        return out.at[:, pl.ds(pl.multiple_of(g * W + (u % 2) * H, H), H), pl.ds((u // 2) * W, W)]

    def zout(u):
        return [copy(xsend.at[u // 4], urecv.at[u, ZOUT], zbuf.at[u, (g + d) % 4], place(u), dev(dz=d)) for d in (2, 1, 3)]

    def own_out(u):
        return pltpu.make_async_copy(zbuf.at[u, g], place(u), osem.at[u])

    def e3(u):
        take(urecv.at[u, A2], 384)

        @pl.loop(0, NP, unroll=4)
        def _(p):
            a = (s - shifts[p] + 32) % 32
            zbuf[u, p // 4, p % 4] = yf[u][a // 8, (a // 2) % 4, a % 2]

        start(zout(u))
        own_out(u).start()

    barrier = pltpu.get_barrier_semaphore()
    peers = ([dev(dz=d) for d in (1, 2, 3)] + [dev(dy=d) for d in (1, 2, 3)]
             + [dev(dx=d) for d in (1, 2, 3)] + [SB])
    for to in peers:
        pl.semaphore_signal(barrier, inc=1, device_id=to, device_id_type=MESH)

    def right_copy(i):
        cols = pl.ds(i * W, W)
        return pltpu.make_async_copy(right.at[:, cols], rmask.at[:, cols], lsem.at[i])

    left_copy = Copy(lambda: pltpu.make_async_copy(left, lmask, lsem.at[C]))
    for i in range(C):
        right_copy(i).start()
    left_copy.start()

    for k in range(4):
        psi_copy(k).start()

    own = dims[s]
    rows = lax.broadcasted_iota(jnp.int32, (M, W), 0)
    cols = lax.broadcasted_iota(jnp.int32, (M, W), 1)

    def masked(ref, i):
        live = (rows < own) & (cols + i * W < own)
        return jnp.where(live, ref[:, i * W:(i + 1) * W].astype(F32), 0.0).astype(BF16)

    def own_right(i):
        right_copy(i).wait()
        r = masked(rmask, i)
        rmask[:, i * W:(i + 1) * W] = r
        rall[i][y // 2, y % 2, x // 2, x % 2, c] = r

    own_right(0)
    pl.semaphore_wait(barrier, len(peers))
    g0(0)
    for i in range(1, C):
        own_right(i)
    next_right().start()
    pltpu.make_async_copy(left, lmask, lsem.at[C]).wait()
    for i in range(C):
        lmask[:, i * W:(i + 1) * W] = masked(lmask, i)

    def slot_of(k):
        r = jnp.int32(0)
        for p in range(NP):
            r = jnp.where(shifts[p] == k, jnp.int32(p), r)
        return r

    pa, pb = slot_of(0), slot_of(1 + 30 * c)
    low, high = jnp.minimum(pa, pb), jnp.maximum(pa, pb)
    place_of[0] = low
    place_of[1] = high
    place_of[2] = pa
    place_of[3] = pb

    @pl.loop(0, 32)
    def _(k):
        p = slot_of(k)
        r = p - (p > low).astype(jnp.int32) - (p > high).astype(jnp.int32)
        r = jnp.where(p == pa, jnp.int32(NR), r)
        inv[k] = jnp.where(p == pb, jnp.int32(NR + 1), r)

    order = (
        (g1, 0), (s0, 0), (g2, 0), (lp, 1), (ga, 0), (lp, 3), (g3, 0), (g0, 1), (s1, 0),
        (lp, 2), (g4, 0), (g1, 1), (lp, 0), (g0, 3), (pr, 0), (s2, 0), (g2, 1), (g0, 2),
        (ga, 1), (ps, 0), (g3, 1), (ad, 0), (g1, 2), (g4, 1), (g2, 2), (ad, 1), (g1, 3),
        (pr, 1), (fi, 0), (ps, 1), (ga, 2), (g3, 2), (g2, 3), (ad, 2), (ga, 3), (g4, 2),
        (e1, 0), (fi, 1), (g3, 3), (ad, 3), (pr, 2), (ps, 2), (fi, 2), (e1, 1), (g4, 3),
        (e2, 0), (fi, 3), (e2, 1), (ad, 4), (pr, 3), (e1, 3), (e1, 2), (ad, 5), (fi, 4),
        (e1, 4), (ps, 3), (e2, 3), (fi, 5), (ad, 6), (e3, 0), (e2, 4), (e1, 5), (ad, 7),
        (e2, 2), (e3, 3), (e2, 5), (fi, 6), (e1, 6), (e3, 1), (fi, 7), (e1, 7), (e3, 5),
        (e3, 4), (e3, 2), (e2, 6), (e2, 7), (e3, 6), (e3, 7),
    )
    for step, i in order:
        step(i)

    for u in range(U):
        take(urecv.at[u, ZOUT], 192)
        own_out(u).wait()
    for i in range(C):
        take(gsend.at[i], 3968, False)
    for k in range(2):
        take(xsend.at[k], 4864, False)
    take(xsend.at[2], 512, False)
    take(rsend.at[U], 768, False)


def body(psi_blocks, left_env, right_env, shifts, sector_dims):
    smem = pl.BlockSpec(memory_space=pltpu.SMEM)
    hbm = pl.BlockSpec(memory_space=pl.ANY)
    out = pl.pallas_call(
        kernel,
        name="sigma",
        out_shape=pltpu.VMEM((4, M, M), BF16),
        in_specs=[smem, smem, hbm, hbm, hbm],
        out_specs=pl.BlockSpec(memory_space=pltpu.VMEM),
        scratch_shapes=[
            pltpu.VMEM((NP, M, M), BF16),
            pltpu.VMEM((M, M), BF16),
            pltpu.VMEM((M, M), BF16),
            pltpu.VMEM((M, M), BF16),
            pltpu.VMEM((M, M), BF16),
            pltpu.VMEM((2, 4, NR, W, W), BF16),
            pltpu.VMEM((4, 2, C, W, W), BF16),
            pltpu.VMEM((U, 6, HALF, H, W), BF16),
            pltpu.VMEM((6, C, W, W), BF16),
            pltpu.VMEM((NP, H, W), BF16),
            pltpu.VMEM((2, C, W, W), BF16),
            pltpu.VMEM((U, 2, 4, 4, H, W), BF16),
            pltpu.VMEM((U, 4, 4, H, W), BF16),
            pltpu.VMEM((U, 4, 2, 4, Q, W), BF16),
            pltpu.VMEM((U, 4, 2, 4, Q, W), BF16),
            pltpu.VMEM((U, 4, 4, H, W), BF16),
            pltpu.SMEM((32,), jnp.int32),
            pltpu.SMEM((4,), jnp.int32),
            pltpu.SemaphoreType.DMA((4,)),
            pltpu.SemaphoreType.DMA((C + 1,)),
            pltpu.SemaphoreType.DMA((U,)),
            pltpu.SemaphoreType.DMA((C,)),
            pltpu.SemaphoreType.DMA((C, GATHER)),
            pltpu.SemaphoreType.DMA((U + 1,)),
            pltpu.SemaphoreType.DMA((3,)),
            pltpu.SemaphoreType.DMA((U + 1, UNIT)),
            *[pltpu.VMEM((2, 2, 2, 2, 2, M, W), BF16)] * C,
            *[pltpu.VMEM((4, 4, 2, H, W), BF16)] * U,
        ],
        compiler_params=pltpu.CompilerParams(
            collective_id=1, has_side_effects=True, vmem_limit_bytes=60 << 20),
        cost_estimate=pl.CostEstimate(flops=2 * 32 * M ** 3, bytes_accessed=12 << 20, transcendentals=0),
    )(shifts, sector_dims, psi_blocks[0], left_env[0, 0], right_env[0, 0])
    return out[None]


def solution(mesh):
    in_specs = (
        P("sec", None, None, None),
        P("ops", "sec", None, None),
        P("ops", "sec", None, None),
        P(),
        P(),
    )
    out_specs = P("sec", "ops", None, None)
    return jax.shard_map(body, mesh=mesh, in_specs=in_specs, out_specs=out_specs, check_vma=False)
```

```python
import jax
import jax.numpy as jnp
from jax import lax
from jax.experimental import pallas as pl
from jax.experimental.pallas import tpu as pltpu
from jax.sharding import PartitionSpec as P

MESH = pl.DeviceIdType.MESH
BF16 = jnp.bfloat16
F32 = jnp.float32

M = 512
W = 128
C = M // W
NP = 16
H = W // 2
Q = H // 2
U = 2 * C
NR = NP - 2
HALF = NR // 2

AG0, AG1, AG2, AG2C, AG3, SIB = range(6)
GATHER = 6
RS, RSB, RSC, SWAP, A1, A2, ZOUT = range(7)
UNIT = 7


class Copy:
    def __init__(self, make):
        self.make = make

    def start(self):
        self.make().start()

    def wait_recv(self):
        self.make().wait_recv()


def start(cs):
    for cp in cs:
        cp.start()


def kernel(shifts, dims, psi, left, right, out,
           inter, early, lmask, rmask, rnext, part, part0, rsin, rsin0, sigma, sigma0,
           v, w, x0, x1, zbuf, inv, place_of,
           psem, lsem, osem, gsend, grecv, rsend, xsend, urecv, *chunked):
    rall, yf = chunked[:C], chunked[C:]
    g = lax.axis_index("ops")
    s = lax.axis_index("sec")
    y, x, c = s // 8, (s // 2) % 4, s % 2

    def dev(dz=0, dy=0, dx=0, dc=0):
        return ((g + dz) % 4, ((y + dy) % 4) * 8 + ((x + dx) % 4) * 2 + (c + dc) % 2)

    SB = dev(dc=1)

    def copy(send, recv, src, dst, to):
        return Copy(lambda: pltpu.make_async_remote_copy(
            src_ref=src, dst_ref=dst, send_sem=send, recv_sem=recv, device_id=to, device_id_type=MESH))

    def take(sem, kib, received=True):
        n = next(n for n in range(1, NP + 1) if kib <= n * M and kib % (16 * n) == 0)
        view = inter.at[pl.ds(0, n), pl.ds(0, kib // n)]
        cp = pltpu.make_async_remote_copy(
            src_ref=view, dst_ref=view, send_sem=sem, recv_sem=sem, device_id=SB, device_id_type=MESH)
        if received:
            cp.wait_recv()
        else:
            cp.wait_send()

    gp, gm, go = (g + 1) % 4, (g + 3) % 4, (g + 2) % 4
    xp, xm, xo = (x + 1) % 4, (x + 3) % 4, (x + 2) % 4
    yp, ym, yo = (y + 1) % 4, (y + 3) % 4, (y + 2) % 4
    XP, XM, YP, YM = dev(dx=1), dev(dx=3), dev(dy=1), dev(dy=3)
    ZP, ZM = dev(dz=1), dev(dz=3)

    def tile(i, yy, xx, first, count):
        return rall[i].at[yy // 2, yy % 2, xx // 2, xx % 2, c, pl.ds(first, count)]

    def row(i, yy, kind, first, count):
        yh, yl = yy // 2, yy % 2
        if kind == "all":
            return rall[i].at[yh, yl, :, :, c, pl.ds(first, count)]
        return rall[i].at[yh, yl, :, (x + 1) % 2, c, pl.ds(first, count)]

    def col(i, xx, kind, first, count):
        xh, xl = xx // 2, xx % 2
        if kind == "all":
            return rall[i].at[:, :, xh, xl, c, pl.ds(first, count)]
        return rall[i].at[:, (y + 1) % 2, xh, xl, c, pl.ds(first, count)]

    def four(i, e, refs, to):
        return [copy(gsend.at[i], grecv.at[i, e], r, r, d) for r, d in zip(refs, to)]

    def ag0(i):
        a, b = tile(i, y, x, 0, 256), tile(i, y, x, 256, 256)
        return four(i, AG0, (a, a, b, b), (XP, XM, YP, YM))

    def ag1(i):
        return four(i, AG1, (tile(i, y, xm, 0, 128), tile(i, y, xp, 128, 128),
                             tile(i, ym, x, 256, 128), tile(i, yp, x, 384, 128)), (XP, XM, YP, YM))

    def ag2a(i):
        a, b = tile(i, y, x, 0, 256), tile(i, y, x, 256, 256)
        return four(i, AG2, (a, a, b, b), (YP, YM, XP, XM))

    def ag2b(i):
        a, b = row(i, y, "near", 0, 256), col(i, x, "near", 256, 256)
        return four(i, AG2, (a, a, b, b), (YP, YM, XP, XM))

    def ag2c(i):
        a, b = tile(i, y, xo, 0, 256), tile(i, yo, x, 256, 256)
        return four(i, AG2C, (a, a, b, b), (YP, YM, XP, XM))

    def ag3a(i):
        return four(i, AG3, (tile(i, ym, x, 0, 128), tile(i, yp, x, 128, 128),
                             tile(i, y, xm, 256, 128), tile(i, y, xp, 384, 128)), (YP, YM, XP, XM))

    def ag3b(i):
        return four(i, AG3, (row(i, ym, "near", 0, 128), row(i, yp, "near", 128, 128),
                                 col(i, xm, "near", 256, 128), col(i, xp, "near", 384, 128)),
                    (YP, YM, XP, XM))

    def ag3c(i):
        return four(i, AG3, (tile(i, ym, xo, 0, 128), tile(i, yp, xo, 128, 128),
                                 tile(i, yo, xm, 256, 128), tile(i, yo, xp, 384, 128)),
                    (YP, YM, XP, XM))

    def sib(i):
        refs = (row(i, y, "all", 0, 256), col(i, x, "all", 256, 256),
                rall[i].at[:, (y + 1) % 2, :, :, c, pl.ds(0, 256)],
                rall[i].at[:, :, :, (x + 1) % 2, c, pl.ds(256, 256)],
                row(i, yo, "all", 0, 256), col(i, xo, "all", 256, 256))
        return [copy(gsend.at[i], grecv.at[i, SIB], r, r, SB) for r in refs]

    def g0(i):
        start(ag0(i) + ag2a(i))

    def g1(i):
        take(grecv.at[i, AG0], 256)
        start(ag1(i) + ag2b(i))

    def g2(i):
        take(grecv.at[i, AG1], 128)
        start(ag2c(i) + sib(i)[:2])

    def ga(i):
        take(grecv.at[i, AG2], 768)
        start(ag3a(i) + ag3b(i))

    def g3(i):
        take(grecv.at[i, AG2C], 256)
        start(ag3c(i) + sib(i)[2:4])

    def g4(i):
        take(grecv.at[i, AG3], 512)
        start(sib(i)[4:])

    def psi_copy(k):
        four_blocks = pl.ds(4 * k, 4)
        return pltpu.make_async_copy(psi.at[four_blocks], inter.at[four_blocks], psem.at[k])

    def lp(i):
        @pl.loop(4 * i, 4 * i + 4)
        def _(p):
            inter[p] = jnp.dot(lmask[...], inter[p], preferred_element_type=F32).astype(BF16)

    def passes(u, send_a, send_b, into):
        def to(e, k, src, device):
            return copy(rsend.at[u], urecv.at[u, e], src, into(k), device)

        return [to(RS, 0, send_a(go), ZM), to(RSB, 1, send_b(go), ZP),
                to(RSC, 2, send_a(gp), ZP), to(RSC, 3, send_b(gm), ZM),
                to(RSC, 4, send_a(gm), ZM), to(RSC, 5, send_b(gp), ZP)]

    def rs(u):
        b, r = (u // 2) % 2, pl.ds((u % 2) * H, H)
        return passes(u, lambda d: part.at[b, d, pl.ds(0, HALF), r], lambda d: part.at[b, d, pl.ds(HALF, HALF), r],
                      lambda k: rsin.at[u, k])

    def rs0():
        return passes(U, lambda d: part0.at[d, 0], lambda d: part0.at[d, 1], lambda k: rsin0.at[k])

    def products(i, first):
        b = i % 2

        @pl.loop(first, first + HALF, unroll=HALF)
        def _(j):
            p = j + (j >= place_of[0]).astype(jnp.int32)
            p = p + (p >= place_of[1]).astype(jnp.int32)
            t = (s + shifts[p]) % 32
            r = jnp.dot(inter[p], rall[i][t // 16, (t // 8) % 2, (t // 4) % 2, (t // 2) % 2, t % 2],
                        preferred_element_type=F32).astype(BF16)
            for d in range(4):
                part[b, d, j] = r[d * W:(d + 1) * W]

    def pr(i):
        take(grecv.at[i, SIB], 2048)
        cs = rs(2 * i)
        products(i, 0)
        start([cs[0], cs[2]])
        products(i, HALF)
        start([cs[1], cs[3]])

    def ps(i):
        start(rs(2 * i + 1)[:4])

    def ad(u):
        b, r = (u // 2) % 2, slice((u % 2) * H, (u % 2) * H + H)
        cs = rs(u)
        for k, d, first in ((0, gm, 0), (1, gp, HALF)):
            cs[k].wait_recv()

            @pl.loop(0, HALF, unroll=HALF)
            def _(j):
                part[b, d, first + j, r] = (part[b, d, first + j, r].astype(F32)
                                            + rsin[u, k, j].astype(F32)).astype(BF16)

            cs[4 + k].start()

    def swap(u):
        return copy(xsend.at[u // 4], urecv.at[u, SWAP], w.at[u], v.at[u, c], SB)

    def fi(u):
        i, r = u // 2, slice((u % 2) * H, (u % 2) * H + H)
        b = i % 2
        take(urecv.at[u, RSC], 448)

        @pl.loop(0, HALF, unroll=HALF)
        def _(j):
            sigma[j] = (part[b, g, j, r].astype(F32) + rsin[u, 2, j].astype(F32)
                        + rsin[u, 4, j].astype(F32)).astype(BF16)
            sigma[j + HALF] = (part[b, g, j + HALF, r].astype(F32) + rsin[u, 3, j].astype(F32)
                               + rsin[u, 5, j].astype(F32)).astype(BF16)

        sigma[NR] = sigma0[0, i, r]
        sigma[NR + 1] = sigma0[1, i, r]

        @pl.loop(0, 16, unroll=4)
        def _(t):
            ty, tx = t // 4, t % 4
            base = ty * 8 + tx * 2 - s + 32
            w[u, ty, tx] = sigma[inv[(base + (c + 1) % 2) % 32]]
            v[u, c, ty, tx] = sigma[inv[(base + c) % 32]]

        swap(u).start()
        take(rsend.at[u], 672, False)

    def next_right():
        return copy(xsend.at[2], urecv.at[U, SWAP], rmask, rnext, SB)

    def s0(_):
        for k in range(4):
            psi_copy(k).wait()

        cs = rs0()
        for k, ref in ((0, rmask), (1, rnext)):
            if k:
                next_right().wait_recv()
            early[...] = jnp.dot(lmask[...], inter[place_of[2 + k]], preferred_element_type=F32).astype(BF16)
            r = jnp.dot(early[...], ref[...], preferred_element_type=F32).astype(BF16)
            for d in range(4):
                for i in range(C):
                    part0[d, k, i] = r[d * W:(d + 1) * W, i * W:(i + 1) * W]
            start([cs[k], cs[2 + k]])

    def s1(_):
        cs = rs0()
        for k, d in ((0, gm), (1, gp)):
            cs[k].wait_recv()
            for i in range(C):
                part0[d, k, i] = (part0[d, k, i].astype(F32) + rsin0[k, i].astype(F32)).astype(BF16)
            cs[4 + k].start()

    def s2(_):
        take(urecv.at[U, RSC], 512)
        for k in range(2):
            for i in range(C):
                sigma0[k, i] = (part0[g, k, i].astype(F32) + rsin0[2 + k, i].astype(F32)
                                + rsin0[4 + k, i].astype(F32)).astype(BF16)

    def a1(u):
        cs = []
        for d in (1, 3, 2):
            tx, ty = (x + d) % 4, (y + d) % 4
            cs.append(copy(xsend.at[u // 4], urecv.at[u, A1], v.at[u, :, :, tx, pl.ds(0, Q)], x0.at[u, x], dev(dx=d)))
            cs.append(copy(xsend.at[u // 4], urecv.at[u, A1], v.at[u, :, ty, :, pl.ds(Q, Q)], x1.at[u, y], dev(dy=d)))
        return cs

    def a2(u):
        cs = []
        for d in (1, 3, 2):
            tx, ty = (x + d) % 4, (y + d) % 4
            cs.append(copy(xsend.at[u // 4], urecv.at[u, A2], x0.at[u, :, :, ty], yf[u].at[y, :, :, pl.ds(0, Q)], dev(dy=d)))
            cs.append(copy(xsend.at[u // 4], urecv.at[u, A2], x1.at[u, :, :, tx], yf[u].at[:, x, :, pl.ds(Q, Q)], dev(dx=d)))
        return cs

    def e1(u):
        swap(u).wait_recv()
        start(a1(u))
        for k in range(4):
            for q in range(2):
                x0[u, x, q, k] = v[u, q, k, x, pl.ds(0, Q)]
                x1[u, y, q, k] = v[u, q, y, k, pl.ds(Q, Q)]

    def e2(u):
        take(urecv.at[u, A1], 384)
        start(a2(u))
        for k in range(4):
            for q in range(2):
                yf[u][y, k, q, pl.ds(0, Q)] = x0[u, k, q, y]
                yf[u][k, x, q, pl.ds(Q, Q)] = x1[u, k, q, x]

    def place(u):
        return out.at[:, pl.ds(pl.multiple_of(g * W + (u % 2) * H, H), H), pl.ds((u // 2) * W, W)]

    def zout(u):
        return [copy(xsend.at[u // 4], urecv.at[u, ZOUT], zbuf.at[u, (g + d) % 4], place(u), dev(dz=d)) for d in (2, 1, 3)]

    def own_out(u):
        return pltpu.make_async_copy(zbuf.at[u, g], place(u), osem.at[u])

    def e3(u):
        take(urecv.at[u, A2], 384)

        @pl.loop(0, NP, unroll=4)
        def _(p):
            a = (s - shifts[p] + 32) % 32
            zbuf[u, p // 4, p % 4] = yf[u][a // 8, (a // 2) % 4, a % 2]

        start(zout(u))
        own_out(u).start()

    barrier = pltpu.get_barrier_semaphore()
    peers = ([dev(dz=d) for d in (1, 2, 3)] + [dev(dy=d) for d in (1, 2, 3)]
             + [dev(dx=d) for d in (1, 2, 3)] + [SB])
    for to in peers:
        pl.semaphore_signal(barrier, inc=1, device_id=to, device_id_type=MESH)

    def right_copy(i):
        cols = pl.ds(i * W, W)
        return pltpu.make_async_copy(right.at[:, cols], rmask.at[:, cols], lsem.at[i])

    left_copy = Copy(lambda: pltpu.make_async_copy(left, lmask, lsem.at[C]))
    for i in range(C):
        right_copy(i).start()
    left_copy.start()

    for k in range(4):
        psi_copy(k).start()

    own = dims[s]
    rows = lax.broadcasted_iota(jnp.int32, (M, W), 0)
    cols = lax.broadcasted_iota(jnp.int32, (M, W), 1)

    def masked(ref, i):
        live = (rows < own) & (cols + i * W < own)
        return jnp.where(live, ref[:, i * W:(i + 1) * W].astype(F32), 0.0).astype(BF16)

    def own_right(i):
        right_copy(i).wait()
        r = masked(rmask, i)
        rmask[:, i * W:(i + 1) * W] = r
        rall[i][y // 2, y % 2, x // 2, x % 2, c] = r

    own_right(0)
    pl.semaphore_wait(barrier, len(peers))
    g0(0)
    for i in range(1, C):
        own_right(i)
    next_right().start()
    pltpu.make_async_copy(left, lmask, lsem.at[C]).wait()
    for i in range(C):
        lmask[:, i * W:(i + 1) * W] = masked(lmask, i)

    def slot_of(k):
        r = jnp.int32(0)
        for p in range(NP):
            r = jnp.where(shifts[p] == k, jnp.int32(p), r)
        return r

    pa, pb = slot_of(0), slot_of(1 + 30 * c)
    low, high = jnp.minimum(pa, pb), jnp.maximum(pa, pb)
    place_of[0] = low
    place_of[1] = high
    place_of[2] = pa
    place_of[3] = pb

    @pl.loop(0, 32)
    def _(k):
        p = slot_of(k)
        r = p - (p > low).astype(jnp.int32) - (p > high).astype(jnp.int32)
        r = jnp.where(p == pa, jnp.int32(NR), r)
        inv[k] = jnp.where(p == pb, jnp.int32(NR + 1), r)

    order = (
        (s0, 0), (g1, 0), (lp, 0), (g2, 0), (lp, 1), (ga, 0), (lp, 2), (g3, 0), (g0, 1),
        (s1, 0), (lp, 3), (g4, 0), (g0, 2), (g1, 1), (pr, 0), (g2, 1), (ps, 0), (ga, 1),
        (g3, 1), (ad, 0), (g1, 2), (g4, 1), (s2, 0), (g0, 3), (g2, 2), (ad, 1), (pr, 1),
        (g1, 3), (ga, 2), (ps, 1), (fi, 0), (g3, 2), (g2, 3), (ga, 3), (fi, 1), (e1, 0),
        (ad, 2), (g4, 2), (ad, 3), (pr, 2), (fi, 2), (g3, 3), (e1, 1), (e1, 2), (fi, 3),
        (ps, 2), (g4, 3), (e2, 1), (ad, 4), (e1, 3), (e2, 2), (ad, 5), (pr, 3), (fi, 4),
        (ps, 3), (fi, 5), (e1, 4), (e1, 5), (e2, 0), (ad, 6), (ad, 7), (e2, 3), (e3, 2),
        (e2, 5), (fi, 6), (e3, 1), (e3, 0), (e1, 6), (fi, 7), (e2, 4), (e1, 7), (e2, 6),
        (e3, 3), (e3, 4), (e2, 7), (e3, 5), (e3, 6), (e3, 7),
    )
    for step, i in order:
        step(i)

    for u in range(U):
        take(urecv.at[u, ZOUT], 192)
        own_out(u).wait()
    for i in range(C):
        take(gsend.at[i], 3968, False)
    for k in range(2):
        take(xsend.at[k], 4864, False)
    take(xsend.at[2], 512, False)
    take(rsend.at[U], 768, False)


def body(psi_blocks, left_env, right_env, shifts, sector_dims):
    smem = pl.BlockSpec(memory_space=pltpu.SMEM)
    hbm = pl.BlockSpec(memory_space=pl.ANY)
    out = pl.pallas_call(
        kernel,
        name="sigma",
        out_shape=pltpu.VMEM((4, M, M), BF16),
        in_specs=[smem, smem, hbm, hbm, hbm],
        out_specs=pl.BlockSpec(memory_space=pltpu.VMEM),
        scratch_shapes=[
            pltpu.VMEM((NP, M, M), BF16),
            pltpu.VMEM((M, M), BF16),
            pltpu.VMEM((M, M), BF16),
            pltpu.VMEM((M, M), BF16),
            pltpu.VMEM((M, M), BF16),
            pltpu.VMEM((2, 4, NR, W, W), BF16),
            pltpu.VMEM((4, 2, C, W, W), BF16),
            pltpu.VMEM((U, 6, HALF, H, W), BF16),
            pltpu.VMEM((6, C, W, W), BF16),
            pltpu.VMEM((NP, H, W), BF16),
            pltpu.VMEM((2, C, W, W), BF16),
            pltpu.VMEM((U, 2, 4, 4, H, W), BF16),
            pltpu.VMEM((U, 4, 4, H, W), BF16),
            pltpu.VMEM((U, 4, 2, 4, Q, W), BF16),
            pltpu.VMEM((U, 4, 2, 4, Q, W), BF16),
            pltpu.VMEM((U, 4, 4, H, W), BF16),
            pltpu.SMEM((32,), jnp.int32),
            pltpu.SMEM((4,), jnp.int32),
            pltpu.SemaphoreType.DMA((4,)),
            pltpu.SemaphoreType.DMA((C + 1,)),
            pltpu.SemaphoreType.DMA((U,)),
            pltpu.SemaphoreType.DMA((C,)),
            pltpu.SemaphoreType.DMA((C, GATHER)),
            pltpu.SemaphoreType.DMA((U + 1,)),
            pltpu.SemaphoreType.DMA((3,)),
            pltpu.SemaphoreType.DMA((U + 1, UNIT)),
            *[pltpu.VMEM((2, 2, 2, 2, 2, M, W), BF16)] * C,
            *[pltpu.VMEM((4, 4, 2, H, W), BF16)] * U,
        ],
        compiler_params=pltpu.CompilerParams(
            collective_id=1, has_side_effects=True, vmem_limit_bytes=60 << 20),
        cost_estimate=pl.CostEstimate(flops=2 * 32 * M ** 3, bytes_accessed=12 << 20, transcendentals=0),
    )(shifts, sector_dims, psi_blocks[0], left_env[0, 0], right_env[0, 0])
    return out[None]


def solution(mesh):
    in_specs = (
        P("sec", None, None, None),
        P("ops", "sec", None, None),
        P("ops", "sec", None, None),
        P(),
        P(),
    )
    out_specs = P("sec", "ops", None, None)
    return jax.shard_map(body, mesh=mesh, in_specs=in_specs, out_specs=out_specs, check_vma=False)
```

```python
import jax
import jax.numpy as jnp
from jax import lax
from jax.experimental import pallas as pl
from jax.experimental.pallas import tpu as pltpu
from jax.sharding import PartitionSpec as P

MESH = pl.DeviceIdType.MESH
BF16 = jnp.bfloat16
F32 = jnp.float32

M = 512
W = 128
C = M // W
NP = 16
H = W // 2
Q = H // 2
U = 2 * C
NR = NP - 2
HALF = NR // 2

AG0, AG1, AG2, AG2C, AG3, AG3C, SIB = range(7)
GATHER = 7
RS, RSB, RSC, SWAP, A1, A2, ZOUT = range(7)
UNIT = 7


class Copy:
    def __init__(self, make):
        self.make = make

    def start(self):
        self.make().start()

    def wait_recv(self):
        self.make().wait_recv()


def start(cs):
    for cp in cs:
        cp.start()


def kernel(shifts, dims, psi, left, right, out,
           inter, early, lmask, rmask, rnext, part, part0, rsin, rsin0, sigma, sigma0,
           v, w, x0, x1, zbuf, inv, place_of,
           psem, lsem, osem, gsend, grecv, rsend, xsend, urecv, *chunked):
    rall, yf = chunked[:C], chunked[C:]
    g = lax.axis_index("ops")
    s = lax.axis_index("sec")
    y, x, c = s // 8, (s // 2) % 4, s % 2

    def dev(dz=0, dy=0, dx=0, dc=0):
        return ((g + dz) % 4, ((y + dy) % 4) * 8 + ((x + dx) % 4) * 2 + (c + dc) % 2)

    SB = dev(dc=1)

    def copy(send, recv, src, dst, to):
        return Copy(lambda: pltpu.make_async_remote_copy(
            src_ref=src, dst_ref=dst, send_sem=send, recv_sem=recv, device_id=to, device_id_type=MESH))

    def take(sem, kib, received=True):
        n = next(n for n in range(1, NP + 1) if kib <= n * M and kib % (16 * n) == 0)
        view = inter.at[pl.ds(0, n), pl.ds(0, kib // n)]
        cp = pltpu.make_async_remote_copy(
            src_ref=view, dst_ref=view, send_sem=sem, recv_sem=sem, device_id=SB, device_id_type=MESH)
        if received:
            cp.wait_recv()
        else:
            cp.wait_send()

    gp, gm, go = (g + 1) % 4, (g + 3) % 4, (g + 2) % 4
    xp, xm, xo = (x + 1) % 4, (x + 3) % 4, (x + 2) % 4
    yp, ym, yo = (y + 1) % 4, (y + 3) % 4, (y + 2) % 4
    XP, XM, YP, YM = dev(dx=1), dev(dx=3), dev(dy=1), dev(dy=3)
    ZP, ZM = dev(dz=1), dev(dz=3)

    def tile(i, yy, xx, first, count):
        return rall[i].at[yy // 2, yy % 2, xx // 2, xx % 2, c, pl.ds(first, count)]

    def row(i, yy, kind, first, count):
        yh, yl = yy // 2, yy % 2
        if kind == "all":
            return rall[i].at[yh, yl, :, :, c, pl.ds(first, count)]
        return rall[i].at[yh, yl, :, (x + 1) % 2, c, pl.ds(first, count)]

    def col(i, xx, kind, first, count):
        xh, xl = xx // 2, xx % 2
        if kind == "all":
            return rall[i].at[:, :, xh, xl, c, pl.ds(first, count)]
        return rall[i].at[:, (y + 1) % 2, xh, xl, c, pl.ds(first, count)]

    def four(i, e, refs, to):
        return [copy(gsend.at[i], grecv.at[i, e], r, r, d) for r, d in zip(refs, to)]

    def ag0(i):
        a, b = tile(i, y, x, 0, 256), tile(i, y, x, 256, 256)
        return four(i, AG0, (a, a, b, b), (XP, XM, YP, YM))

    def ag1(i):
        return four(i, AG1, (tile(i, y, xm, 0, 128), tile(i, y, xp, 128, 128),
                             tile(i, ym, x, 256, 128), tile(i, yp, x, 384, 128)), (XP, XM, YP, YM))

    def ag2a(i):
        a, b = tile(i, y, x, 0, 256), tile(i, y, x, 256, 256)
        return four(i, AG2, (a, a, b, b), (YP, YM, XP, XM))

    def ag2b(i):
        a, b = row(i, y, "near", 0, 256), col(i, x, "near", 256, 256)
        return four(i, AG2, (a, a, b, b), (YP, YM, XP, XM))

    def ag2c(i):
        a, b = tile(i, y, xo, 0, 256), tile(i, yo, x, 256, 256)
        return four(i, AG2C, (a, a, b, b), (YP, YM, XP, XM))

    def ag3a(i):
        return four(i, AG3, (tile(i, ym, x, 0, 128), tile(i, yp, x, 128, 128),
                             tile(i, y, xm, 256, 128), tile(i, y, xp, 384, 128)), (YP, YM, XP, XM))

    def ag3b(i):
        return four(i, AG3, (row(i, ym, "near", 0, 128), row(i, yp, "near", 128, 128),
                                 col(i, xm, "near", 256, 128), col(i, xp, "near", 384, 128)),
                    (YP, YM, XP, XM))

    def ag3c(i):
        return four(i, AG3C, (tile(i, ym, xo, 0, 128), tile(i, yp, xo, 128, 128),
                                 tile(i, yo, xm, 256, 128), tile(i, yo, xp, 384, 128)),
                    (YP, YM, XP, XM))

    def sib(i, *refs):
        start([copy(gsend.at[i], grecv.at[i, SIB], r, r, SB) for r in refs])

    def g0(i):
        start(ag0(i) + ag2a(i))

    def g1(i):
        take(grecv.at[i, AG0], 256)
        start(ag1(i) + ag2b(i))

    def g2(i):
        take(grecv.at[i, AG1], 128)
        start(ag2c(i))
        sib(i, row(i, y, "all", 0, 256), col(i, x, "all", 256, 256))

    def ga(i):
        take(grecv.at[i, AG2], 768)
        start(ag3a(i) + ag3b(i))
        sib(i, rall[i].at[:, (y + 1) % 2, x // 2, x % 2, c, pl.ds(0, 256)],
            rall[i].at[y // 2, y % 2, :, (x + 1) % 2, c, pl.ds(256, 256)],
            rall[i].at[:, (y + 1) % 2, :, (x + 1) % 2, c])

    def g3(i):
        take(grecv.at[i, AG2C], 256)
        start(ag3c(i))
        sib(i, rall[i].at[:, (y + 1) % 2, xo // 2, xo % 2, c, pl.ds(0, 256)],
            rall[i].at[yo // 2, yo % 2, :, (x + 1) % 2, c, pl.ds(256, 256)])

    def gb(i):
        take(grecv.at[i, AG3], 384)
        sib(i, tile(i, yo, x, 0, 256), row(i, yo, "near", 0, 256),
            tile(i, y, xo, 256, 256), col(i, xo, "near", 256, 256))

    def g4(i):
        take(grecv.at[i, AG3C], 128)
        sib(i, tile(i, yo, xo, 0, 512))

    def psi_copy(k):
        four_blocks = pl.ds(4 * k, 4)
        return pltpu.make_async_copy(psi.at[four_blocks], inter.at[four_blocks], psem.at[k])

    def lp(i):
        @pl.loop(4 * i, 4 * i + 4, unroll=2)
        def _(p):
            inter[p] = jnp.dot(lmask[...], inter[p], preferred_element_type=F32).astype(BF16)

    def passes(u, send_a, send_b, into):
        def to(e, k, src, device):
            return copy(rsend.at[u], urecv.at[u, e], src, into(k), device)

        return [to(RS, 0, send_a(go), ZM), to(RSB, 1, send_b(go), ZP),
                to(RSC, 2, send_a(gp), ZP), to(RSC, 3, send_b(gm), ZM),
                to(RSC, 4, send_a(gm), ZM), to(RSC, 5, send_b(gp), ZP)]

    def rs(u):
        b, h = (u // 2) % 2, u % 2
        return passes(u, lambda d: part.at[b, d, h, pl.ds(0, HALF)], lambda d: part.at[b, d, h, pl.ds(HALF, HALF)],
                      lambda k: rsin.at[u, k])

    def rs0():
        return passes(U, lambda d: part0.at[d, 0], lambda d: part0.at[d, 1], lambda k: rsin0.at[k])

    def products(i, first):
        b = i % 2

        @pl.loop(first, first + HALF, unroll=HALF)
        def _(j):
            p = j + (j >= place_of[0]).astype(jnp.int32)
            p = p + (p >= place_of[1]).astype(jnp.int32)
            t = (s + shifts[p]) % 32
            r = jnp.dot(inter[p], rall[i][t // 16, (t // 8) % 2, (t // 4) % 2, (t // 2) % 2, t % 2],
                        preferred_element_type=F32).astype(BF16)
            for d in range(4):
                for h in range(2):
                    part[b, d, h, j] = r[d * W + h * H:d * W + (h + 1) * H]

    def pr(i):
        take(grecv.at[i, SIB], 2048)
        cs = rs(2 * i)
        products(i, 0)
        start([cs[0], cs[2]])
        products(i, HALF)
        start([cs[1], cs[3]])

    def ps(i):
        start(rs(2 * i + 1)[:4])

    def ad(u):
        b, h = (u // 2) % 2, u % 2
        cs = rs(u)
        for k, d, first in ((0, gm, 0), (1, gp, HALF)):
            cs[k].wait_recv()

            @pl.loop(0, HALF, unroll=HALF)
            def _(j):
                part[b, d, h, first + j] = (part[b, d, h, first + j].astype(F32)
                                            + rsin[u, k, j].astype(F32)).astype(BF16)

            cs[4 + k].start()

    def swap(u):
        return copy(xsend.at[u // 4], urecv.at[u, SWAP], w.at[u], v.at[u, c], SB)

    def fi(u):
        i, r = u // 2, slice((u % 2) * H, (u % 2) * H + H)
        b, h = i % 2, u % 2
        take(urecv.at[u, RSC], 448)

        @pl.loop(0, HALF, unroll=HALF)
        def _(j):
            sigma[j] = (part[b, g, h, j].astype(F32) + rsin[u, 2, j].astype(F32)
                        + rsin[u, 4, j].astype(F32)).astype(BF16)
            sigma[j + HALF] = (part[b, g, h, j + HALF].astype(F32) + rsin[u, 3, j].astype(F32)
                               + rsin[u, 5, j].astype(F32)).astype(BF16)

        sigma[NR] = sigma0[0, i, r]
        sigma[NR + 1] = sigma0[1, i, r]

        @pl.loop(0, 16, unroll=4)
        def _(t):
            ty, tx = t // 4, t % 4
            base = ty * 8 + tx * 2 - s + 32
            w[u, ty, tx] = sigma[inv[(base + (c + 1) % 2) % 32]]
            v[u, c, ty, tx] = sigma[inv[(base + c) % 32]]

        swap(u).start()
        take(rsend.at[u], 672, False)

    def next_right():
        return copy(xsend.at[2], urecv.at[U, SWAP], rmask, rnext, SB)

    def s0(_):
        for k in range(4):
            psi_copy(k).wait()

        cs = rs0()
        for k, ref in ((0, rmask), (1, rnext)):
            if k:
                next_right().wait_recv()
            early[...] = jnp.dot(lmask[...], inter[place_of[2 + k]], preferred_element_type=F32).astype(BF16)
            r = jnp.dot(early[...], ref[...], preferred_element_type=F32).astype(BF16)
            for d in range(4):
                for i in range(C):
                    part0[d, k, i] = r[d * W:(d + 1) * W, i * W:(i + 1) * W]
            start([cs[k], cs[2 + k]])

    def s1(_):
        cs = rs0()
        for k, d in ((0, gm), (1, gp)):
            cs[k].wait_recv()
            for i in range(C):
                part0[d, k, i] = (part0[d, k, i].astype(F32) + rsin0[k, i].astype(F32)).astype(BF16)
            cs[4 + k].start()

    def s2(_):
        take(urecv.at[U, RSC], 512)
        for k in range(2):
            for i in range(C):
                sigma0[k, i] = (part0[g, k, i].astype(F32) + rsin0[2 + k, i].astype(F32)
                                + rsin0[4 + k, i].astype(F32)).astype(BF16)

    def a1(u):
        cs = []
        for d in (1, 3, 2):
            tx, ty = (x + d) % 4, (y + d) % 4
            cs.append(copy(xsend.at[u // 4], urecv.at[u, A1], v.at[u, :, :, tx, pl.ds(0, Q)], x0.at[u, x], dev(dx=d)))
            cs.append(copy(xsend.at[u // 4], urecv.at[u, A1], v.at[u, :, ty, :, pl.ds(Q, Q)], x1.at[u, y], dev(dy=d)))
        return cs

    def a2(u):
        cs = []
        for d in (1, 3, 2):
            tx, ty = (x + d) % 4, (y + d) % 4
            cs.append(copy(xsend.at[u // 4], urecv.at[u, A2], x0.at[u, :, :, ty], yf[u].at[y, :, :, pl.ds(0, Q)], dev(dy=d)))
            cs.append(copy(xsend.at[u // 4], urecv.at[u, A2], x1.at[u, :, :, tx], yf[u].at[:, x, :, pl.ds(Q, Q)], dev(dx=d)))
        return cs

    def e1(u):
        swap(u).wait_recv()
        start(a1(u))
        for k in range(4):
            for q in range(2):
                x0[u, x, q, k] = v[u, q, k, x, pl.ds(0, Q)]
                x1[u, y, q, k] = v[u, q, y, k, pl.ds(Q, Q)]

    def e2(u):
        take(urecv.at[u, A1], 384)
        start(a2(u))
        for k in range(4):
            for q in range(2):
                yf[u][y, k, q, pl.ds(0, Q)] = x0[u, k, q, y]
                yf[u][k, x, q, pl.ds(Q, Q)] = x1[u, k, q, x]

    def place(u):
        return out.at[:, pl.ds(pl.multiple_of(g * W + (u % 2) * H, H), H), pl.ds((u // 2) * W, W)]

    def zout(u):
        return [copy(xsend.at[u // 4], urecv.at[u, ZOUT], zbuf.at[u, (g + d) % 4], place(u), dev(dz=d)) for d in (2, 1, 3)]

    def own_out(u):
        return pltpu.make_async_copy(zbuf.at[u, g], place(u), osem.at[u])

    def e3(u):
        take(urecv.at[u, A2], 384)

        @pl.loop(0, NP, unroll=4)
        def _(p):
            a = (s - shifts[p] + 32) % 32
            zbuf[u, p // 4, p % 4] = yf[u][a // 8, (a // 2) % 4, a % 2]

        start(zout(u))
        own_out(u).start()

    barrier = pltpu.get_barrier_semaphore()
    peers = ([dev(dz=d) for d in (1, 2, 3)] + [dev(dy=d) for d in (1, 2, 3)]
             + [dev(dx=d) for d in (1, 2, 3)] + [SB])
    for to in peers:
        pl.semaphore_signal(barrier, inc=1, device_id=to, device_id_type=MESH)

    def right_copy(i):
        cols = pl.ds(i * W, W)
        return pltpu.make_async_copy(right.at[:, cols], rmask.at[:, cols], lsem.at[i])

    left_copy = Copy(lambda: pltpu.make_async_copy(left, lmask, lsem.at[C]))
    for i in range(C):
        right_copy(i).start()
    left_copy.start()

    for k in range(4):
        psi_copy(k).start()

    own = dims[s]
    rows = lax.broadcasted_iota(jnp.int32, (M, W), 0)
    cols = lax.broadcasted_iota(jnp.int32, (M, W), 1)

    def masked(ref, i):
        live = (rows < own) & (cols + i * W < own)
        return jnp.where(live, ref[:, i * W:(i + 1) * W].astype(F32), 0.0).astype(BF16)

    def own_right(i):
        right_copy(i).wait()
        r = masked(rmask, i)
        rmask[:, i * W:(i + 1) * W] = r
        rall[i][y // 2, y % 2, x // 2, x % 2, c] = r

    own_right(0)
    pl.semaphore_wait(barrier, len(peers))
    g0(0)
    for i in range(1, C):
        own_right(i)
    next_right().start()
    pltpu.make_async_copy(left, lmask, lsem.at[C]).wait()
    for i in range(C):
        lmask[:, i * W:(i + 1) * W] = masked(lmask, i)

    def slot_of(k):
        r = jnp.int32(0)
        for p in range(NP):
            r = jnp.where(shifts[p] == k, jnp.int32(p), r)
        return r

    pa, pb = slot_of(0), slot_of(1 + 30 * c)
    low, high = jnp.minimum(pa, pb), jnp.maximum(pa, pb)
    place_of[0] = low
    place_of[1] = high
    place_of[2] = pa
    place_of[3] = pb

    def tb(_):
        @pl.loop(0, 32)
        def _(k):
            p = slot_of(k)
            r = p - (p > low).astype(jnp.int32) - (p > high).astype(jnp.int32)
            r = jnp.where(p == pa, jnp.int32(NR), r)
            inv[k] = jnp.where(p == pb, jnp.int32(NR + 1), r)

    order = (
        (s0, 0), (g1, 0), (lp, 0), (g2, 0), (lp, 1), (ga, 0), (lp, 2), (g3, 0), (g0, 1),
        (s1, 0), (lp, 3), (gb, 0), (g4, 0), (g0, 2), (g1, 1), (pr, 0), (tb, 0), (g2, 1), (ps, 0),
        (ga, 1), (g3, 1), (ad, 0), (g1, 2), (gb, 1), (g4, 1), (s2, 0), (g0, 3), (g2, 2),
        (ad, 1), (pr, 1), (g1, 3), (ga, 2), (ps, 1), (fi, 0), (g3, 2), (g2, 3), (ga, 3),
        (fi, 1), (e1, 0), (ad, 2), (gb, 2), (g4, 2), (ad, 3), (pr, 2), (fi, 2), (g3, 3),
        (e1, 1), (e1, 2), (fi, 3), (ps, 2), (gb, 3), (g4, 3), (e2, 1), (ad, 4), (e1, 3),
        (e2, 2), (ad, 5), (pr, 3), (fi, 4), (ps, 3), (fi, 5), (e1, 4), (e1, 5), (e2, 0),
        (ad, 6), (ad, 7), (e2, 3), (e3, 2), (e2, 5), (fi, 6), (e3, 1), (e3, 0), (e1, 6),
        (fi, 7), (e2, 4), (e1, 7), (e2, 6), (e3, 3), (e3, 4), (e2, 7), (e3, 5), (e3, 6),
        (e3, 7),
    )
    for step, i in order:
        step(i)

    for u in range(U):
        take(urecv.at[u, ZOUT], 192)
        own_out(u).wait()
    for i in range(C):
        take(gsend.at[i], 3968, False)
    for k in range(2):
        take(xsend.at[k], 4864, False)
    take(xsend.at[2], 512, False)
    take(rsend.at[U], 768, False)


def body(psi_blocks, left_env, right_env, shifts, sector_dims):
    smem = pl.BlockSpec(memory_space=pltpu.SMEM)
    hbm = pl.BlockSpec(memory_space=pl.ANY)
    out = pl.pallas_call(
        kernel,
        name="sigma",
        out_shape=pltpu.VMEM((4, M, M), BF16),
        in_specs=[smem, smem, hbm, hbm, hbm],
        out_specs=pl.BlockSpec(memory_space=pltpu.VMEM),
        scratch_shapes=[
            pltpu.VMEM((NP, M, M), BF16),
            pltpu.VMEM((M, M), BF16),
            pltpu.VMEM((M, M), BF16),
            pltpu.VMEM((M, M), BF16),
            pltpu.VMEM((M, M), BF16),
            pltpu.VMEM((2, 4, 2, NR, H, W), BF16),
            pltpu.VMEM((4, 2, C, W, W), BF16),
            pltpu.VMEM((U, 6, HALF, H, W), BF16),
            pltpu.VMEM((6, C, W, W), BF16),
            pltpu.VMEM((NP, H, W), BF16),
            pltpu.VMEM((2, C, W, W), BF16),
            pltpu.VMEM((U, 2, 4, 4, H, W), BF16),
            pltpu.VMEM((U, 4, 4, H, W), BF16),
            pltpu.VMEM((U, 4, 2, 4, Q, W), BF16),
            pltpu.VMEM((U, 4, 2, 4, Q, W), BF16),
            pltpu.VMEM((U, 4, 4, H, W), BF16),
            pltpu.SMEM((32,), jnp.int32),
            pltpu.SMEM((4,), jnp.int32),
            pltpu.SemaphoreType.DMA((4,)),
            pltpu.SemaphoreType.DMA((C + 1,)),
            pltpu.SemaphoreType.DMA((U,)),
            pltpu.SemaphoreType.DMA((C,)),
            pltpu.SemaphoreType.DMA((C, GATHER)),
            pltpu.SemaphoreType.DMA((U + 1,)),
            pltpu.SemaphoreType.DMA((3,)),
            pltpu.SemaphoreType.DMA((U + 1, UNIT)),
            *[pltpu.VMEM((2, 2, 2, 2, 2, M, W), BF16)] * C,
            *[pltpu.VMEM((4, 4, 2, H, W), BF16)] * U,
        ],
        compiler_params=pltpu.CompilerParams(
            collective_id=1, has_side_effects=True, vmem_limit_bytes=60 << 20),
        cost_estimate=pl.CostEstimate(flops=2 * 32 * M ** 3, bytes_accessed=12 << 20, transcendentals=0),
    )(shifts, sector_dims, psi_blocks[0], left_env[0, 0], right_env[0, 0])
    return out[None]


def solution(mesh):
    in_specs = (
        P("sec", None, None, None),
        P("ops", "sec", None, None),
        P("ops", "sec", None, None),
        P(),
        P(),
    )
    out_specs = P("sec", "ops", None, None)
    return jax.shard_map(body, mesh=mesh, in_specs=in_specs, out_specs=out_specs, check_vma=False)
```

```python
import jax
import jax.numpy as jnp
from jax import lax
from jax.experimental import pallas as pl
from jax.experimental.pallas import tpu as pltpu
from jax.sharding import PartitionSpec as P

MESH = pl.DeviceIdType.MESH
BF16 = jnp.bfloat16
F32 = jnp.float32

M = 512
W = 128
C = M // W
NP = 16
H = W // 2
Q = H // 2
U = 2 * C
NR = NP - 2
HALF = NR // 2

AG0, AG1, AG2, AG2C, AG3, AG3C, SIB = range(7)
GATHER = 7
RS, RSB, RSC, SWAP, A1, A2, ZOUT = range(7)
UNIT = 7


class Copy:
    def __init__(self, make):
        self.make = make

    def start(self):
        self.make().start()

    def wait_recv(self):
        self.make().wait_recv()


def start(cs):
    for cp in cs:
        cp.start()


def kernel(shifts, dims, psi, left, right, out,
           inter, lmask, rmask, rnext, part, part0, rsin, rsin0, sigma, sigma0,
           v, w, x0, x1, zbuf, inv, place_of,
           psem, lsem, osem, gsend, grecv, rsend, xsend, urecv, *chunked):
    rall, yf = chunked[:C], chunked[C:]
    g = lax.axis_index("ops")
    s = lax.axis_index("sec")
    y, x, c = s // 8, (s // 2) % 4, s % 2

    def dev(dz=0, dy=0, dx=0, dc=0):
        return ((g + dz) % 4, ((y + dy) % 4) * 8 + ((x + dx) % 4) * 2 + (c + dc) % 2)

    SB = dev(dc=1)

    def copy(send, recv, src, dst, to):
        return Copy(lambda: pltpu.make_async_remote_copy(
            src_ref=src, dst_ref=dst, send_sem=send, recv_sem=recv, device_id=to, device_id_type=MESH))

    def take(sem, kib, received=True):
        n = next(n for n in range(1, NP + 1) if kib <= n * M and kib % (16 * n) == 0)
        view = inter.at[pl.ds(0, n), pl.ds(0, kib // n)]
        cp = pltpu.make_async_remote_copy(
            src_ref=view, dst_ref=view, send_sem=sem, recv_sem=sem, device_id=SB, device_id_type=MESH)
        if received:
            cp.wait_recv()
        else:
            cp.wait_send()

    gp, gm, go = (g + 1) % 4, (g + 3) % 4, (g + 2) % 4
    xp, xm, xo = (x + 1) % 4, (x + 3) % 4, (x + 2) % 4
    yp, ym, yo = (y + 1) % 4, (y + 3) % 4, (y + 2) % 4
    XP, XM, YP, YM = dev(dx=1), dev(dx=3), dev(dy=1), dev(dy=3)
    ZP, ZM = dev(dz=1), dev(dz=3)

    def tile(i, yy, xx, first, count):
        return rall[i].at[yy // 2, yy % 2, xx // 2, xx % 2, c, pl.ds(first, count)]

    def row(i, yy, kind, first, count):
        yh, yl = yy // 2, yy % 2
        if kind == "all":
            return rall[i].at[yh, yl, :, :, c, pl.ds(first, count)]
        return rall[i].at[yh, yl, :, (x + 1) % 2, c, pl.ds(first, count)]

    def col(i, xx, kind, first, count):
        xh, xl = xx // 2, xx % 2
        if kind == "all":
            return rall[i].at[:, :, xh, xl, c, pl.ds(first, count)]
        return rall[i].at[:, (y + 1) % 2, xh, xl, c, pl.ds(first, count)]

    def four(i, e, refs, to):
        return [copy(gsend.at[i], grecv.at[i, e], r, r, d) for r, d in zip(refs, to)]

    def ag0(i):
        a, b = tile(i, y, x, 0, 256), tile(i, y, x, 256, 256)
        return four(i, AG0, (a, a, b, b), (XP, XM, YP, YM))

    def ag1(i):
        return four(i, AG1, (tile(i, y, xm, 0, 128), tile(i, y, xp, 128, 128),
                             tile(i, ym, x, 256, 128), tile(i, yp, x, 384, 128)), (XP, XM, YP, YM))

    def ag2a(i):
        a, b = tile(i, y, x, 0, 256), tile(i, y, x, 256, 256)
        return four(i, AG2, (a, a, b, b), (YP, YM, XP, XM))

    def ag2b(i):
        a, b = row(i, y, "near", 0, 256), col(i, x, "near", 256, 256)
        return four(i, AG2, (a, a, b, b), (YP, YM, XP, XM))

    def ag2c(i):
        a, b = tile(i, y, xo, 0, 256), tile(i, yo, x, 256, 256)
        return four(i, AG2C, (a, a, b, b), (YP, YM, XP, XM))

    def ag3a(i):
        return four(i, AG3, (tile(i, ym, x, 0, 128), tile(i, yp, x, 128, 128),
                             tile(i, y, xm, 256, 128), tile(i, y, xp, 384, 128)), (YP, YM, XP, XM))

    def ag3b(i):
        return four(i, AG3, (row(i, ym, "near", 0, 128), row(i, yp, "near", 128, 128),
                                 col(i, xm, "near", 256, 128), col(i, xp, "near", 384, 128)),
                    (YP, YM, XP, XM))

    def ag3c(i):
        return four(i, AG3C, (tile(i, ym, xo, 0, 128), tile(i, yp, xo, 128, 128),
                                 tile(i, yo, xm, 256, 128), tile(i, yo, xp, 384, 128)),
                    (YP, YM, XP, XM))

    def sib(i, *refs):
        start([copy(gsend.at[i], grecv.at[i, SIB], r, r, SB) for r in refs])

    def g0(i):
        start(ag0(i) + ag2a(i))

    def g1(i):
        take(grecv.at[i, AG0], 256)
        start(ag1(i) + ag2b(i))

    def g2(i):
        take(grecv.at[i, AG1], 128)
        start(ag2c(i))
        sib(i, row(i, y, "all", 0, 256), col(i, x, "all", 256, 256))

    def ga(i):
        take(grecv.at[i, AG2], 768)
        start(ag3a(i) + ag3b(i))
        sib(i, rall[i].at[:, (y + 1) % 2, x // 2, x % 2, c, pl.ds(0, 256)],
            rall[i].at[y // 2, y % 2, :, (x + 1) % 2, c, pl.ds(256, 256)],
            rall[i].at[:, (y + 1) % 2, :, (x + 1) % 2, c])

    def g3(i):
        take(grecv.at[i, AG2C], 256)
        start(ag3c(i))
        sib(i, rall[i].at[:, (y + 1) % 2, xo // 2, xo % 2, c, pl.ds(0, 256)],
            rall[i].at[yo // 2, yo % 2, :, (x + 1) % 2, c, pl.ds(256, 256)])

    def gb(i):
        take(grecv.at[i, AG3], 384)
        sib(i, tile(i, yo, x, 0, 256), row(i, yo, "near", 0, 256),
            tile(i, y, xo, 256, 256), col(i, xo, "near", 256, 256))

    def g4(i):
        take(grecv.at[i, AG3C], 128)
        sib(i, tile(i, yo, xo, 0, 512))

    def psi_copy(k):
        four_blocks = pl.ds(4 * k, 4)
        return pltpu.make_async_copy(psi.at[four_blocks], inter.at[four_blocks], psem.at[k])

    def lp(i):
        psi_copy(i).wait()

        @pl.loop(4 * i, 4 * i + 4, unroll=2)
        def _(p):
            inter[p] = jnp.dot(lmask[...], inter[p], preferred_element_type=F32).astype(BF16)

    def passes(u, send_a, send_b, into):
        def to(e, k, src, device):
            return copy(rsend.at[u], urecv.at[u, e], src, into(k), device)

        return [to(RS, 0, send_a(go), ZM), to(RSB, 1, send_b(go), ZP),
                to(RSC, 2, send_a(gp), ZP), to(RSC, 3, send_b(gm), ZM),
                to(RSC, 4, send_a(gm), ZM), to(RSC, 5, send_b(gp), ZP)]

    def rs(u):
        b, h = (u // 2) % 2, u % 2
        return passes(u, lambda d: part.at[b, d, h, pl.ds(0, HALF)], lambda d: part.at[b, d, h, pl.ds(HALF, HALF)],
                      lambda k: rsin.at[u, k])

    def rs0():
        return passes(U, lambda d: part0.at[d, 0], lambda d: part0.at[d, 1], lambda k: rsin0.at[k])

    def products(i, first):
        b = i % 2

        @pl.loop(first, first + HALF, unroll=HALF)
        def _(j):
            p = j + (j >= place_of[0]).astype(jnp.int32)
            p = p + (p >= place_of[1]).astype(jnp.int32)
            t = (s + shifts[p]) % 32
            r = jnp.dot(inter[p], rall[i][t // 16, (t // 8) % 2, (t // 4) % 2, (t // 2) % 2, t % 2],
                        preferred_element_type=F32).astype(BF16)
            for d in range(4):
                for h in range(2):
                    part[b, d, h, j] = r[d * W + h * H:d * W + (h + 1) * H]

    def pr(i):
        take(grecv.at[i, SIB], 2048)
        cs = rs(2 * i)
        products(i, 0)
        start([cs[0], cs[2]])
        products(i, HALF)
        start([cs[1], cs[3]])

    def ps(i):
        start(rs(2 * i + 1)[:4])

    def ad(u):
        b, h = (u // 2) % 2, u % 2
        cs = rs(u)
        for k, d, first in ((0, gm, 0), (1, gp, HALF)):
            cs[k].wait_recv()

            @pl.loop(0, HALF, unroll=HALF)
            def _(j):
                part[b, d, h, first + j] = (part[b, d, h, first + j].astype(F32)
                                            + rsin[u, k, j].astype(F32)).astype(BF16)

            cs[4 + k].start()

    def swap(u):
        return copy(xsend.at[u // 4], urecv.at[u, SWAP], w.at[u], v.at[u, c], SB)

    def fi(u):
        i, r = u // 2, slice((u % 2) * H, (u % 2) * H + H)
        b, h = i % 2, u % 2
        take(urecv.at[u, RSC], 448)

        @pl.loop(0, HALF, unroll=HALF)
        def _(j):
            sigma[j] = (part[b, g, h, j].astype(F32) + rsin[u, 2, j].astype(F32)
                        + rsin[u, 4, j].astype(F32)).astype(BF16)
            sigma[j + HALF] = (part[b, g, h, j + HALF].astype(F32) + rsin[u, 3, j].astype(F32)
                               + rsin[u, 5, j].astype(F32)).astype(BF16)

        sigma[NR] = sigma0[0, i, r]
        sigma[NR + 1] = sigma0[1, i, r]

        @pl.loop(0, 16, unroll=4)
        def _(t):
            ty, tx = t // 4, t % 4
            base = ty * 8 + tx * 2 - s + 32
            w[u, ty, tx] = sigma[inv[(base + (c + 1) % 2) % 32]]
            v[u, c, ty, tx] = sigma[inv[(base + c) % 32]]

        swap(u).start()
        take(rsend.at[u], 672, False)

    def next_right():
        return copy(xsend.at[2], urecv.at[U, SWAP], rmask, rnext, SB)

    def s0(_):
        cs = rs0()
        for k, ref in ((0, rmask), (1, rnext)):
            if k:
                next_right().wait_recv()
            r = jnp.dot(inter[place_of[2 + k]], ref[...], preferred_element_type=F32).astype(BF16)
            for d in range(4):
                for i in range(C):
                    part0[d, k, i] = r[d * W:(d + 1) * W, i * W:(i + 1) * W]
            start([cs[k], cs[2 + k]])

    def s1(_):
        cs = rs0()
        for k, d in ((0, gm), (1, gp)):
            cs[k].wait_recv()
            for i in range(C):
                part0[d, k, i] = (part0[d, k, i].astype(F32) + rsin0[k, i].astype(F32)).astype(BF16)
            cs[4 + k].start()

    def s2(_):
        take(urecv.at[U, RSC], 512)
        for k in range(2):
            for i in range(C):
                sigma0[k, i] = (part0[g, k, i].astype(F32) + rsin0[2 + k, i].astype(F32)
                                + rsin0[4 + k, i].astype(F32)).astype(BF16)

    def a1(u):
        cs = []
        for d in (1, 3, 2):
            tx, ty = (x + d) % 4, (y + d) % 4
            cs.append(copy(xsend.at[u // 4], urecv.at[u, A1], v.at[u, :, :, tx, pl.ds(0, Q)], x0.at[u, x], dev(dx=d)))
            cs.append(copy(xsend.at[u // 4], urecv.at[u, A1], v.at[u, :, ty, :, pl.ds(Q, Q)], x1.at[u, y], dev(dy=d)))
        return cs

    def a2(u):
        cs = []
        for d in (1, 3, 2):
            tx, ty = (x + d) % 4, (y + d) % 4
            cs.append(copy(xsend.at[u // 4], urecv.at[u, A2], x0.at[u, :, :, ty], yf[u].at[y, :, :, pl.ds(0, Q)], dev(dy=d)))
            cs.append(copy(xsend.at[u // 4], urecv.at[u, A2], x1.at[u, :, :, tx], yf[u].at[:, x, :, pl.ds(Q, Q)], dev(dx=d)))
        return cs

    def e1(u):
        swap(u).wait_recv()
        start(a1(u))
        for k in range(4):
            for q in range(2):
                x0[u, x, q, k] = v[u, q, k, x, pl.ds(0, Q)]
                x1[u, y, q, k] = v[u, q, y, k, pl.ds(Q, Q)]

    def e2(u):
        take(urecv.at[u, A1], 384)
        start(a2(u))
        for k in range(4):
            for q in range(2):
                yf[u][y, k, q, pl.ds(0, Q)] = x0[u, k, q, y]
                yf[u][k, x, q, pl.ds(Q, Q)] = x1[u, k, q, x]

    def place(u):
        return out.at[:, pl.ds(pl.multiple_of(g * W + (u % 2) * H, H), H), pl.ds((u // 2) * W, W)]

    def zout(u):
        return [copy(xsend.at[u // 4], urecv.at[u, ZOUT], zbuf.at[u, (g + d) % 4], place(u), dev(dz=d)) for d in (2, 1, 3)]

    def own_out(u):
        return pltpu.make_async_copy(zbuf.at[u, g], place(u), osem.at[u])

    def e3(u):
        take(urecv.at[u, A2], 384)

        @pl.loop(0, NP, unroll=4)
        def _(p):
            a = (s - shifts[p] + 32) % 32
            zbuf[u, p // 4, p % 4] = yf[u][a // 8, (a // 2) % 4, a % 2]

        start(zout(u))
        own_out(u).start()

    barrier = pltpu.get_barrier_semaphore()
    peers = ([dev(dz=d) for d in (1, 2, 3)] + [dev(dy=d) for d in (1, 2, 3)]
             + [dev(dx=d) for d in (1, 2, 3)] + [SB])
    for to in peers:
        pl.semaphore_signal(barrier, inc=1, device_id=to, device_id_type=MESH)

    def right_copy(i):
        cols = pl.ds(i * W, W)
        return pltpu.make_async_copy(right.at[:, cols], rmask.at[:, cols], lsem.at[i])

    left_copy = Copy(lambda: pltpu.make_async_copy(left, lmask, lsem.at[C]))
    for i in range(C):
        right_copy(i).start()
    left_copy.start()

    for k in range(4):
        psi_copy(k).start()

    own = dims[s]
    rows = lax.broadcasted_iota(jnp.int32, (M, W), 0)
    cols = lax.broadcasted_iota(jnp.int32, (M, W), 1)

    def masked(ref, i):
        live = (rows < own) & (cols + i * W < own)
        return jnp.where(live, ref[:, i * W:(i + 1) * W].astype(F32), 0.0).astype(BF16)

    def own_right(i):
        right_copy(i).wait()
        r = masked(rmask, i)
        rmask[:, i * W:(i + 1) * W] = r
        rall[i][y // 2, y % 2, x // 2, x % 2, c] = r

    own_right(0)
    pl.semaphore_wait(barrier, len(peers))
    g0(0)
    for i in range(1, C):
        own_right(i)
    next_right().start()
    pltpu.make_async_copy(left, lmask, lsem.at[C]).wait()
    for i in range(C):
        lmask[:, i * W:(i + 1) * W] = masked(lmask, i)

    def slot_of(k):
        r = jnp.int32(0)
        for p in range(NP):
            r = jnp.where(shifts[p] == k, jnp.int32(p), r)
        return r

    pa, pb = slot_of(0), slot_of(1 + 30 * c)
    low, high = jnp.minimum(pa, pb), jnp.maximum(pa, pb)
    place_of[0] = low
    place_of[1] = high
    place_of[2] = pa
    place_of[3] = pb

    def tb(_):
        @pl.loop(0, 32)
        def _(k):
            p = slot_of(k)
            r = p - (p > low).astype(jnp.int32) - (p > high).astype(jnp.int32)
            r = jnp.where(p == pa, jnp.int32(NR), r)
            inv[k] = jnp.where(p == pb, jnp.int32(NR + 1), r)

    order = (
        (g1, 0), (lp, 0), (lp, 1), (g2, 0), (lp, 2), (ga, 0), (lp, 3), (s0, 0), (g3, 0),
        (g0, 1), (gb, 0), (g4, 0), (s1, 0), (g0, 2), (g1, 1), (pr, 0), (tb, 0), (g2, 1),
        (ps, 0), (ga, 1), (g3, 1), (ad, 0), (g1, 2), (gb, 1), (g4, 1), (s2, 0), (g0, 3),
        (g2, 2), (ad, 1), (pr, 1), (g1, 3), (ga, 2), (ps, 1), (fi, 0), (g3, 2), (g2, 3),
        (ga, 3), (fi, 1), (e1, 0), (ad, 2), (gb, 2), (g4, 2), (ad, 3), (pr, 2), (fi, 2),
        (g3, 3), (e1, 1), (e1, 2), (fi, 3), (ps, 2), (gb, 3), (g4, 3), (e2, 1), (ad, 4),
        (e1, 3), (e2, 2), (ad, 5), (pr, 3), (fi, 4), (ps, 3), (fi, 5), (e1, 4), (e1, 5),
        (e2, 0), (ad, 6), (ad, 7), (e2, 3), (e3, 2), (e2, 5), (fi, 6), (e3, 1), (e3, 0),
        (e1, 6), (fi, 7), (e2, 4), (e1, 7), (e2, 6), (e3, 3), (e3, 4), (e2, 7), (e3, 5),
        (e3, 6), (e3, 7),
    )
    for step, i in order:
        step(i)

    for u in range(U):
        take(urecv.at[u, ZOUT], 192)
        own_out(u).wait()
    for i in range(C):
        take(gsend.at[i], 3968, False)
    for k in range(2):
        take(xsend.at[k], 4864, False)
    take(xsend.at[2], 512, False)
    take(rsend.at[U], 768, False)


def body(psi_blocks, left_env, right_env, shifts, sector_dims):
    smem = pl.BlockSpec(memory_space=pltpu.SMEM)
    hbm = pl.BlockSpec(memory_space=pl.ANY)
    out = pl.pallas_call(
        kernel,
        name="sigma",
        out_shape=pltpu.VMEM((4, M, M), BF16),
        in_specs=[smem, smem, hbm, hbm, hbm],
        out_specs=pl.BlockSpec(memory_space=pltpu.VMEM),
        scratch_shapes=[
            pltpu.VMEM((NP, M, M), BF16),
            pltpu.VMEM((M, M), BF16),
            pltpu.VMEM((M, M), BF16),
            pltpu.VMEM((M, M), BF16),
            pltpu.VMEM((2, 4, 2, NR, H, W), BF16),
            pltpu.VMEM((4, 2, C, W, W), BF16),
            pltpu.VMEM((U, 6, HALF, H, W), BF16),
            pltpu.VMEM((6, C, W, W), BF16),
            pltpu.VMEM((NP, H, W), BF16),
            pltpu.VMEM((2, C, W, W), BF16),
            pltpu.VMEM((U, 2, 4, 4, H, W), BF16),
            pltpu.VMEM((U, 4, 4, H, W), BF16),
            pltpu.VMEM((U, 4, 2, 4, Q, W), BF16),
            pltpu.VMEM((U, 4, 2, 4, Q, W), BF16),
            pltpu.VMEM((U, 4, 4, H, W), BF16),
            pltpu.SMEM((32,), jnp.int32),
            pltpu.SMEM((4,), jnp.int32),
            pltpu.SemaphoreType.DMA((4,)),
            pltpu.SemaphoreType.DMA((C + 1,)),
            pltpu.SemaphoreType.DMA((U,)),
            pltpu.SemaphoreType.DMA((C,)),
            pltpu.SemaphoreType.DMA((C, GATHER)),
            pltpu.SemaphoreType.DMA((U + 1,)),
            pltpu.SemaphoreType.DMA((3,)),
            pltpu.SemaphoreType.DMA((U + 1, UNIT)),
            *[pltpu.VMEM((2, 2, 2, 2, 2, M, W), BF16)] * C,
            *[pltpu.VMEM((4, 4, 2, H, W), BF16)] * U,
        ],
        compiler_params=pltpu.CompilerParams(
            collective_id=1, has_side_effects=True, vmem_limit_bytes=60 << 20),
        cost_estimate=pl.CostEstimate(flops=2 * 32 * M ** 3, bytes_accessed=12 << 20, transcendentals=0),
    )(shifts, sector_dims, psi_blocks[0], left_env[0, 0], right_env[0, 0])
    return out[None]


def solution(mesh):
    in_specs = (
        P("sec", None, None, None),
        P("ops", "sec", None, None),
        P("ops", "sec", None, None),
        P(),
        P(),
    )
    out_specs = P("sec", "ops", None, None)
    return jax.shard_map(body, mesh=mesh, in_specs=in_specs, out_specs=out_specs, check_vma=False)
```
